512 devices in a mesh: lib: 32 (over y, x), ctx: 2 (over core), head: 8 (over z).
Axes of the slice: x: 4, y: 8, z: 8, core: 2. Of those that a mesh axis runs over, the one named last changes fastest.
Arguments:
- queries: bfloat16 [32, 128, 8192], P('lib', None, 'head'), may hold values from -50 to 50
- passage_keys: bfloat16 [512, 512, 1024], P('lib', 'ctx', 'head'), may hold values from -6 to 6
- passage_values: bfloat16 [512, 512, 1024], P('lib', 'ctx', 'head'), may hold values from -6 to 6
- offsets: int32 [512], P('lib'), may hold values from 0 to 4095
- out_weight: bfloat16 [8192, 8192], P('head', 'lib'), may hold values from -0.5 to 0.5
- passage_list: int32 [32, 16], P('lib'), may hold values from 0 to 511, as said below
- targets: int32 [32, 16], P('lib'), may hold values from 0 to 8191
- row_counts: int32 [32], P('lib'), may hold values from 1 to 128
Outputs:
- output: bfloat16 [2, 2048, 8192], P('ctx', 'head', 'lib')
The draws below stay inside these ranges and needn't reach their ends.
Inputs may be any that keep to these rules, and one draw needn't show every extreme that they name: `passage_list`: each row names 16 different passages; passage i belongs to owner i // 16; no row names more than 2 passages of one owner, and in every row some owner has exactly 2.
All inputs are finite; a program needn't handle non-finite values.
Results may differ from the reference program's by a relative error of at most 0.012.
The reference program's roundings to bfloat16 on the way count: a program that leaves them out, or rounds other values in their place, can miss the bound.
Values may be sent and summed in bfloat16 or wider, within the bound.
No kernel may reach another device: no remote copies, remote signals or barrier semaphores. Data moves between devices by JAX's collectives and lax.ppermute only.
A program may use at most 64 MiB of HBM per device.

```python
import jax
import jax.numpy as jnp
from jax import lax

D = 8192
HEAD_DIM = 128
BLOCK = 512
LIST = 16
PASS_DEV = 16
ROWS = 128
KV_HEADS = 8
HEADS = 64
PROMPTS = 32
PASSAGES = 512
MOST = 2
N_CTX = 2


def draw_passage_list(key, part):
    slot_count = PROMPTS * MOST
    base = jax.random.fold_in(key, 17)
    first, second, third, fourth = jax.random.split(base, 4)
    popular = jax.random.randint(first, (PROMPTS,), 0, 4) * 262144
    noise = jax.random.randint(second, (PROMPTS, slot_count), 0, 262144)
    favored = jax.random.randint(third, (PROMPTS,), 0, PROMPTS)
    slot_owner = jnp.arange(slot_count, dtype=jnp.int32) // MOST
    boost = jnp.where(slot_owner[None, :] == favored[:, None], 1048576, 0)
    score = (noise + popular[slot_owner][None, :] + boost) * slot_count + jnp.arange(slot_count, dtype=jnp.int32)[None, :]
    unused, picked = lax.top_k(score, LIST)
    picked_owner = picked // MOST
    picked_copy = picked % MOST
    shuffle = jax.random.randint(fourth, (PROMPTS, PROMPTS, PASS_DEV), 0, 1048576) * PASS_DEV
    shuffle = shuffle + jnp.arange(PASS_DEV, dtype=jnp.int32)
    ranking = jnp.argsort(shuffle, axis=-1).astype(jnp.int32)
    within = ranking[jnp.arange(PROMPTS)[:, None], picked_owner, picked_copy]
    return (picked_owner * PASS_DEV + within).astype(jnp.int32)


def draw_queries(key, part):
    shape = (PROMPTS, ROWS, HEADS * HEAD_DIM)
    first = jax.random.fold_in(jax.random.fold_in(key, 23), 0)
    return jnp.clip(2.0 * jax.random.normal(first, shape, jnp.float32), -8.0, 8.0).astype(jnp.bfloat16)


def set_ends(array, own_key, low, high):
    longest = array.shape.index(max(array.shape))
    spots = []
    for shift in (0, 1):
        where = [jax.random.randint(jax.random.fold_in(own_key, axis), (), 0, length) for axis, length in enumerate(array.shape)]
        where[longest] = (where[longest] + shift) % array.shape[longest]
        spots.append(tuple(where))
    return array.at[spots[0]].set(low).at[spots[1]].set(high)


def shard_levels(key, extent, shards, smallest, top_value):
    def one(dim, blocks):
        heights = jax.random.uniform(jax.random.fold_in(jax.random.fold_in(key, 6), dim), (blocks,), jnp.float32, smallest / len(shards), top_value / len(shards))
        return jnp.repeat(jnp.exp(heights), extent[dim] // blocks).reshape((-1,) + (1,) * (len(extent) - dim - 1))

    loudness = one(*shards[0])
    for cut in shards[1:]:
        loudness = loudness * one(*cut)
    return loudness


def scatter_about(rng, shape, scale, limit, cuts=(), kind=jnp.bfloat16):
    values = jax.random.normal(rng, shape, jnp.float32) * scale
    if len(cuts) > 0:
        values = shard_levels(rng, shape, cuts, -0.22, 0.18) * values
    return jnp.clip(values, min=-limit, max=limit).astype(kind)


def setup_inputs(seed: int = 0) -> dict:
    arg_keys = jax.random.split(jax.random.key(seed), 9)
    queries = draw_queries(jax.random.fold_in(arg_keys[8], 71), 0)
    passage_keys = scatter_about(arg_keys[1], (PASSAGES, BLOCK, KV_HEADS * HEAD_DIM), 1.0, 6.0, ((0, 32), (1, 2), (2, 8)))
    passage_values = scatter_about(arg_keys[2], (PASSAGES, BLOCK, KV_HEADS * HEAD_DIM), 1.0, 6.0, ((0, 32), (1, 2), (2, 8)))
    offsets = set_ends(jax.random.randint(arg_keys[3], (PASSAGES,), 0, 8 * BLOCK), jax.random.fold_in(arg_keys[3], 1), 0, (8 * BLOCK) - 1).astype(jnp.int32)
    out_weight = scatter_about(arg_keys[4], (HEADS * HEAD_DIM, D), HEAD_DIM ** -0.5, 0.5, ((0, 8), (1, 32)))
    passage_list = draw_passage_list(jax.random.fold_in(arg_keys[8], 71), 0)
    targets = set_ends(jax.random.randint(arg_keys[6], (PROMPTS, LIST), 0, LIST * BLOCK), jax.random.fold_in(arg_keys[6], 1), 0, (LIST * BLOCK) - 1).astype(jnp.int32)
    row_counts = set_ends(jax.random.randint(arg_keys[7], (PROMPTS,), 1, ROWS + 1), jax.random.fold_in(arg_keys[7], 1), 1, ROWS).astype(jnp.int32)
    return {"queries": queries, "passage_keys": passage_keys, "passage_values": passage_values, "offsets": offsets, "out_weight": out_weight, "passage_list": passage_list, "targets": targets, "row_counts": row_counts}


theta_base = 500000.0


def rotate_keys(block, delta):
    width = block.shape[-1]
    half = width // 2
    inverse = theta_base ** (-2.0 * jnp.arange(half, dtype=jnp.float32) / width)
    angle = delta.astype(jnp.float32)[:, None] * inverse[None, :]
    cosine = jnp.cos(angle)[:, None, :]
    sine = jnp.sin(angle)[:, None, :]
    first = block[..., :half].astype(jnp.float32)
    second = block[..., half:].astype(jnp.float32)
    return jnp.concatenate([first * cosine - second * sine, second * cosine + first * sine], axis=-1)


def partial_softmax(query, keys, values):
    scores = lax.dot_general(query, keys, (((1,), (1,)), ((), ())), preferred_element_type=jnp.float32)
    scores = scores * (query.shape[1] ** -0.5)
    highest = jnp.max(scores, axis=1)
    weights = jnp.exp(scores - highest[:, None])
    totals = jnp.sum(weights, axis=1)
    summed = jnp.dot(weights.astype(jnp.bfloat16), values, preferred_element_type=jnp.float32)
    return highest, totals, summed


def combine(first, second):
    highest = jnp.maximum(first[0], second[0])
    early = jnp.exp(first[0] - highest)
    later = jnp.exp(second[0] - highest)
    return (highest, first[1] * early + second[1] * later,
            first[2] * early[..., None] + second[2] * later[..., None])


def reference(queries, passage_keys, passage_values, offsets, out_weight, passage_list, targets, row_counts):
    group = HEADS // KV_HEADS
    half = BLOCK // N_CTX

    def one_prompt(items):
        query, chosen, target, count = items
        delta = (target - offsets[chosen]).astype(jnp.int32)
        keys = passage_keys[chosen]
        values = passage_values[chosen]

        def one_head(head):
            key_head = lax.dynamic_slice_in_dim(keys, head * HEAD_DIM, HEAD_DIM, 2)
            value_head = lax.dynamic_slice_in_dim(values, head * HEAD_DIM, HEAD_DIM, 2)
            rotated = rotate_keys(key_head, delta).astype(jnp.bfloat16)
            query_rows = lax.dynamic_slice_in_dim(query, head * group * HEAD_DIM, group * HEAD_DIM, 1)
            query_rows = query_rows.reshape(ROWS * group, HEAD_DIM)
            state = None
            for index in range(N_CTX):
                piece_keys = rotated[:, index * half:(index + 1) * half].reshape(LIST * half, HEAD_DIM)
                piece_values = value_head[:, index * half:(index + 1) * half].reshape(LIST * half, HEAD_DIM)
                result = partial_softmax(query_rows, piece_keys, piece_values)
                state = result if state is None else combine(state, result)
            return (state[2] / state[1][:, None]).reshape(ROWS, group * HEAD_DIM)

        heads_out = lax.map(one_head, jnp.arange(KV_HEADS, dtype=jnp.int32))
        attended = jnp.transpose(heads_out, (1, 0, 2)).reshape(ROWS, HEADS * HEAD_DIM)
        live = (jnp.arange(ROWS, dtype=jnp.int32) < count)[:, None]
        return jnp.where(live, attended, jnp.zeros_like(attended)).astype(jnp.bfloat16)

    attended = lax.map(one_prompt, (queries, passage_list, targets, row_counts))

    def project(rows_in):
        return jnp.dot(rows_in, out_weight, preferred_element_type=jnp.float32).astype(jnp.bfloat16)

    projected = lax.map(project, attended)
    halves = projected.reshape(PROMPTS, N_CTX, ROWS // N_CTX, D)
    return jnp.transpose(halves, (1, 0, 2, 3)).reshape(N_CTX, PROMPTS * (ROWS // N_CTX), D)
```

```python
import functools

import jax
import jax.numpy as jnp
from jax import lax
from jax.experimental import pallas as pl
from jax.experimental.pallas import tpu as pltpu
from jax.sharding import Mesh
from jax.sharding import PartitionSpec as P

ROW, COL = "lib_0", "lib_1"
LIB = (ROW, COL)
theta_base = 500000.0
EMPTY = -1e30
CHUNK = 256
MOST = 2


def shift(value, axis, by):
    n = lax.axis_size(axis)
    return lax.ppermute(value, axis, [(i, (i + by) % n) for i in range(n)])


def ring_gather(value, axis):
    n = lax.axis_size(axis)
    pieces = [value] + [None] * (n - 1)
    behind = ahead = value
    for d in range(1, (n + 1) // 2):
        behind = shift(behind, axis, 1)
        ahead = shift(ahead, axis, -1)
        pieces[n - d], pieces[d] = behind, ahead
    if n % 2 == 0:
        half = value.shape[0] // 2
        pieces[n // 2] = jnp.concatenate(
            [shift(behind[:half], axis, 1), shift(ahead[half:], axis, -1)], axis=0
        )
    return pieces


def attend_kernel(scale, slot_ref, q_ref, cos_ref, sin_ref, *refs):
    key_refs, value_refs = refs[:4], refs[4:8]
    out_ref, lse_ref, q_scr, k_scr, s_scr, m_scr, l_scr, acc_scr, used = refs[8:]
    prompt = pl.program_id(0)
    listed = cos_ref.shape[1]
    rows, width = q_ref.shape[1], cos_ref.shape[2]
    group = q_ref.shape[2] // width
    total_rows = rows * group
    held = key_refs[0].shape[0]
    log2e = 1.4426950408889634
    for g in range(group):
        q_scr[g * rows : (g + 1) * rows] = q_ref[0, :, g * width : (g + 1) * width]
    m_scr[...] = jnp.full_like(m_scr, EMPTY)
    l_scr[...] = jnp.zeros_like(l_scr)
    acc_scr[...] = jnp.zeros_like(acc_scr)

    def score(k, count):
        slot = slot_ref[prompt * listed + k]

        @pl.when(slot >= 0)
        def _():
            piece, at = slot // held, slot % held
            for d in range(4):

                @pl.when(piece == d)
                def _():
                    k_scr[...] = key_refs[d][at]

            used[count] = slot
            keys = k_scr[...].astype(jnp.float32)
            cosine = cos_ref[0, pl.ds(k, 1), :]
            sine = sin_ref[0, pl.ds(k, 1), :]
            turned = keys * cosine + pltpu.roll(keys, width // 2, 1) * sine
            turned = turned.astype(jnp.bfloat16)
            for r in range(0, total_rows, CHUNK):
                s = lax.dot_general(
                    q_scr[r : r + CHUNK],
                    turned,
                    (((1,), (1,)), ((), ())),
                    preferred_element_type=jnp.float32,
                )
                s_scr[count, r : r + CHUNK] = s
                highest = m_scr[r : r + CHUNK]
                for t in range(0, s.shape[1], width):
                    highest = jnp.maximum(highest, s[:, t : t + width])
                m_scr[r : r + CHUNK] = highest

        return count + jnp.where(slot >= 0, 1, 0)

    count = lax.fori_loop(0, listed, score, 0)
    for r in range(0, total_rows, CHUNK):
        m = jnp.max(m_scr[r : r + CHUNK], axis=1, keepdims=True)
        m_scr[r : r + CHUNK] = jnp.broadcast_to(m, (CHUNK, width))

    def weigh(t, carry):
        slot = used[t]
        piece, at = slot // held, slot % held
        for d in range(4):

            @pl.when(piece == d)
            def _():
                k_scr[...] = value_refs[d][at]

        for r in range(0, total_rows, CHUNK):
            m = m_scr[r : r + CHUNK]
            s = s_scr[t, r : r + CHUNK]
            parts = [
                jnp.exp2((s[:, u : u + width] - m) * (scale * log2e))
                for u in range(0, s.shape[1], width)
            ]
            l_scr[r : r + CHUNK] += functools.reduce(jnp.add, parts)
            weights = jnp.concatenate(parts, axis=1).astype(jnp.bfloat16)
            acc_scr[r : r + CHUNK] += jnp.dot(
                weights, k_scr[...], preferred_element_type=jnp.float32
            )
        return carry

    lax.fori_loop(0, count, weigh, 0)
    row = lax.broadcasted_iota(jnp.int32, (rows, rows), 0)
    column = lax.broadcasted_iota(jnp.int32, (rows, rows), 1)
    halves = out_ref.shape[0]
    part = rows // halves
    none = count == 0
    for g in range(group):
        span = slice(g * rows, (g + 1) * rows)
        total = jnp.sum(l_scr[span], axis=1, keepdims=True)
        total = jnp.where(none, 1.0, total)
        out = (acc_scr[span] / total).astype(out_ref.dtype)
        for c in range(halves):
            out_ref[c, g, 0] = out[c * part : (c + 1) * part]
        lse = jnp.where(none, EMPTY, m_scr[span] * scale + jnp.log(total))
        lse_ref[0, g : g + 1, :] = jnp.sum(
            jnp.where(row == column, lse, 0.0), axis=0, keepdims=True
        )


def attend(slots, query, cosine, sine, keys, values, halves):
    prompts, rows, features = query.shape
    listed, width = cosine.shape[1:]
    group = features // width
    tokens = keys[0].shape[1]
    most = MOST * len(keys)
    part = rows // halves
    whole = pl.BlockSpec(memory_space=pltpu.VMEM)
    table = pl.BlockSpec((1, listed, width), lambda j, s: (j, 0, 0))
    return pl.pallas_call(
        functools.partial(attend_kernel, width**-0.5),
        out_shape=(
            jax.ShapeDtypeStruct((halves, group, prompts, part, width), jnp.bfloat16),
            jax.ShapeDtypeStruct((prompts, group, rows), jnp.float32),
        ),
        grid_spec=pltpu.PrefetchScalarGridSpec(
            num_scalar_prefetch=1,
            grid=(prompts,),
            in_specs=[pl.BlockSpec((1, rows, features), lambda j, s: (j, 0, 0)), table, table]
            + [whole] * 8,
            out_specs=(
                pl.BlockSpec((halves, group, 1, part, width), lambda j, s: (0, 0, j, 0, 0)),
                pl.BlockSpec((1, group, rows), lambda j, s: (j, 0, 0)),
            ),
            scratch_shapes=[
                pltpu.VMEM((rows * group, width), jnp.bfloat16),
                pltpu.VMEM((tokens, width), jnp.bfloat16),
                pltpu.VMEM((most, rows * group, tokens), jnp.float32),
                pltpu.VMEM((rows * group, width), jnp.float32),
                pltpu.VMEM((rows * group, width), jnp.float32),
                pltpu.VMEM((rows * group, width), jnp.float32),
                pltpu.SMEM((most,), jnp.int32),
            ],
        ),
        compiler_params=pltpu.CompilerParams(vmem_limit_bytes=48 * 1024 * 1024),
    )(slots, query, cosine, sine, *keys, *values)


def project_kernel(columns, where_ref, *refs):
    pieces, weight_ref = refs[:columns], refs[columns]
    out_ref, acc = refs[columns + 1 :]
    step = pl.program_id(0)
    heads, rows = pieces[0].shape[1:3]
    left = jnp.concatenate(
        [jnp.concatenate([p[0, h] for h in range(heads)], axis=1) for p in pieces], axis=0
    )
    right = jnp.concatenate([weight_ref[h, 0] for h in range(heads)], axis=0)
    term = jnp.dot(left, right, preferred_element_type=jnp.float32)

    @pl.when(step == 0)
    def _():
        acc[...] = term

    @pl.when(step > 0)
    def _():
        acc[...] += term

    @pl.when(step == pl.num_programs(0) - 1)
    def _():
        for d in range(columns):
            at = pl.multiple_of(where_ref[pl.num_programs(0) + d] * rows, rows)
            out_ref[pl.ds(at, rows), :] = acc[d * rows : (d + 1) * rows].astype(out_ref.dtype)


def project(where, pieces, weight):
    columns = len(pieces)
    steps, heads, rows, width = pieces[0].shape
    out_columns = weight.shape[-1]
    return pl.pallas_call(
        functools.partial(project_kernel, columns),
        out_shape=jax.ShapeDtypeStruct((columns * rows, out_columns), jnp.bfloat16),
        grid_spec=pltpu.PrefetchScalarGridSpec(
            num_scalar_prefetch=1,
            grid=(steps,),
            in_specs=[pl.BlockSpec((1, heads, rows, width), lambda s, w: (s, 0, 0, 0))] * columns
            + [pl.BlockSpec((heads, 1, width, out_columns), lambda s, w: (0, w[s], 0, 0))],
            out_specs=pl.BlockSpec((columns * rows, out_columns), lambda s, w: (0, 0)),
            scratch_shapes=[pltpu.VMEM((columns * rows, out_columns), jnp.float32)],
        ),
        compiler_params=pltpu.CompilerParams(vmem_limit_bytes=32 * 1024 * 1024),
    )(where, *pieces, weight)


def merged(outs, lses):
    top = jnp.max(lses, axis=0)
    share = jnp.exp(lses - top)
    total = jnp.sum(share, axis=0)
    share = share / total
    out = jnp.sum(outs.astype(jnp.float32) * share[..., None], axis=0)
    return out, top + jnp.log(total)


def three_parts(value):
    first = lax.reduce_precision(value, 8, 7)
    rest = value - first
    second = lax.reduce_precision(rest, 8, 7)
    return jnp.stack([first, second, rest - second]).astype(jnp.bfloat16)


def body(
    queries, passage_keys, passage_values, offsets, out_weight, passage_list, targets, row_counts
):
    rows_of, columns = lax.axis_size(ROW), lax.axis_size(COL)
    y, x, c = lax.axis_index(ROW), lax.axis_index(COL), lax.axis_index("ctx")
    held, tokens, width = passage_keys.shape
    listed = passage_list.shape[1]
    prompt_rows, features = queries.shape[1:]
    group = features // width
    halves = lax.axis_size("ctx")
    half_rows = prompt_rows // halves

    keys = [passage_keys, shift(passage_keys, COL, -1), None, shift(passage_keys, COL, 1)]
    values = [passage_values, shift(passage_values, COL, -1), None, shift(passage_values, COL, 1)]
    keys[2] = shift(keys[3], COL, 1)
    values[2] = shift(values[1], COL, -1)

    asked = jnp.concatenate([passage_list, targets, row_counts[:, None]], axis=1)
    asked = lax.all_gather(asked, ROW, axis=0, tiled=True)
    near_offsets = lax.all_gather(offsets, COL, axis=0, tiled=True)
    query = lax.all_gather(queries, ROW, axis=0, tiled=True)
    weight = lax.all_gather(out_weight, "head", axis=0, tiled=True)

    near = columns * held
    local = asked[:, :listed] - y * near
    mine = (local >= 0) & (local < near)
    ahead = (local // held - x) % columns
    slots = jnp.where(mine, ahead * held + local % held, -1)
    same = local[..., None] == jnp.arange(near, dtype=jnp.int32)
    delta = asked[:, listed : 2 * listed] - jnp.sum(
        jnp.where(same, near_offsets, 0), axis=-1
    )
    half = width // 2
    inverse = theta_base ** (-2.0 * jnp.arange(half, dtype=jnp.float32) / width)
    angle = delta.astype(jnp.float32)[..., None] * inverse
    cosine, sine = jnp.cos(angle), jnp.sin(angle)
    cosine = jnp.concatenate([cosine, cosine], axis=-1)
    sine = jnp.concatenate([-sine, sine], axis=-1)

    out, lse = attend(slots.reshape(-1), query, cosine, sine, keys, values, halves)

    lse = jnp.transpose(lse.reshape(rows_of, group, halves, half_rows), (2, 1, 0, 3))
    swap = [(i, 1 - i) for i in range(2)]
    pick = functools.partial(lax.dynamic_index_in_dim, axis=0, keepdims=False)
    other = lax.ppermute(pick(out, 1 - c), "ctx", swap)
    other_lse = lax.ppermute(pick(lse, 1 - c), "ctx", swap)
    out, lse = merged(
        jnp.stack([pick(out, c), other]), jnp.stack([pick(lse, c), other_lse])
    )

    out = out.astype(jnp.bfloat16).reshape(group, rows_of * half_rows, width)
    parts = jnp.moveaxis(three_parts(lse), 0, 1).reshape(group, -1, width)
    extra = parts.shape[1]
    parts = jnp.pad(parts, ((0, 0), (0, -extra % 16), (0, 0)))
    sent = jnp.concatenate([out, parts], axis=1)
    got = lax.all_to_all(sent, ROW, split_axis=0, concat_axis=0, tiled=True)
    outs = got[:, : rows_of * half_rows].reshape(rows_of, rows_of, half_rows, width)
    lses = got[:, rows_of * half_rows : rows_of * half_rows + extra].astype(jnp.float32)
    lses = jnp.sum(lses.reshape(rows_of, 3, rows_of, half_rows), axis=1)
    attended, _ = merged(outs, lses)
    live = c * half_rows + jnp.arange(half_rows, dtype=jnp.int32) < asked[:, 2 * listed :]
    attended = jnp.where(live[..., None], attended, 0.0).astype(jnp.bfloat16)

    attended = lax.all_to_all(attended, "head", split_axis=0, concat_axis=0, tiled=True)
    pieces = ring_gather(jnp.stack(ring_gather(attended, ROW)), COL)
    where = jnp.concatenate(
        [
            (y + jnp.arange(rows_of, dtype=jnp.int32)) % rows_of,
            (x + jnp.arange(columns, dtype=jnp.int32)) % columns,
        ]
    )
    weight = weight.reshape(lax.axis_size("head"), group, width, -1)
    return project(where, pieces, weight)[None]


def solution(mesh):
    finer = Mesh(
        mesh.devices.reshape(8, 4, mesh.shape["ctx"], mesh.shape["head"]),
        ("lib_0", "lib_1", "ctx", "head"),
    )
    return jax.shard_map(
        body,
        mesh=finer,
        in_specs=(
            P(LIB, None, "head"),
            P(LIB, "ctx", "head"),
            P(LIB, "ctx", "head"),
            P(LIB),
            P("head", LIB),
            P(LIB, None),
            P(LIB, None),
            P(LIB),
        ),
        out_specs=P("ctx", "head", LIB),
        check_vma=False,
    )
```

```python
import functools

import jax
import jax.numpy as jnp
from jax import lax
from jax.experimental import pallas as pl
from jax.experimental.pallas import tpu as pltpu
from jax.sharding import Mesh
from jax.sharding import PartitionSpec as P

ROW, COL = "lib_0", "lib_1"
LIB = (ROW, COL)
theta_base = 500000.0
EMPTY = -1e30
CHUNK = 256
MOST = 2


def shift(value, axis, by):
    n = lax.axis_size(axis)
    return lax.ppermute(value, axis, [(i, (i + by) % n) for i in range(n)])


def far_first(n):
    return sorted(range(1, n), key=lambda d: -min(d, n - d))


def exchange(pieces, axis):
    arrived = list(pieces)
    for d in far_first(len(pieces)):
        arrived[d] = shift(pieces[d], axis, d)
    return arrived


def gather_pieces(value, axis):
    n = lax.axis_size(axis)
    pieces = [value] * n
    for d in far_first(n):
        pieces[d] = shift(value, axis, -d)
    return pieces


def attend_kernel(scale, slot_ref, place_ref, q_ref, cos_ref, sin_ref, *refs):
    key_refs, value_refs = refs[:4], refs[4:8]
    out_ref, lse_ref, q_scr, k_scr, s_scr, m_scr, l_scr, acc_scr, used = refs[8:]
    prompt = pl.program_id(0)
    listed = cos_ref.shape[1]
    rows, width = q_ref.shape[1], cos_ref.shape[2]
    group = q_ref.shape[2] // width
    total_rows = rows * group
    held = key_refs[0].shape[0]
    log2e = 1.4426950408889634
    for g in range(group):
        q_scr[g * rows : (g + 1) * rows] = q_ref[0, :, g * width : (g + 1) * width]
    m_scr[...] = jnp.full_like(m_scr, EMPTY)
    l_scr[...] = jnp.zeros_like(l_scr)
    acc_scr[...] = jnp.zeros_like(acc_scr)

    def score(k, count):
        slot = slot_ref[prompt * listed + k]

        @pl.when(slot >= 0)
        def _():
            piece, at = slot // held, slot % held
            for d in range(4):

                @pl.when(piece == d)
                def _():
                    k_scr[...] = key_refs[d][at]

            used[count] = slot
            keys = k_scr[...].astype(jnp.float32)
            cosine = cos_ref[0, pl.ds(k, 1), :]
            sine = sin_ref[0, pl.ds(k, 1), :]
            turned = keys * cosine + pltpu.roll(keys, width // 2, 1) * sine
            turned = turned.astype(jnp.bfloat16)
            for r in range(0, total_rows, CHUNK):
                s = lax.dot_general(
                    q_scr[r : r + CHUNK],
                    turned,
                    (((1,), (1,)), ((), ())),
                    preferred_element_type=jnp.float32,
                )
                s_scr[count, r : r + CHUNK] = s
                highest = m_scr[r : r + CHUNK]
                for t in range(0, s.shape[1], width):
                    highest = jnp.maximum(highest, s[:, t : t + width])
                m_scr[r : r + CHUNK] = highest

        return count + jnp.where(slot >= 0, 1, 0)

    count = lax.fori_loop(0, listed, score, 0)
    for r in range(0, total_rows, CHUNK):
        m = jnp.max(m_scr[r : r + CHUNK], axis=1, keepdims=True)
        m_scr[r : r + CHUNK] = jnp.broadcast_to(m, (CHUNK, width))

    def weigh(t, carry):
        slot = used[t]
        piece, at = slot // held, slot % held
        for d in range(4):

            @pl.when(piece == d)
            def _():
                k_scr[...] = value_refs[d][at]

        for r in range(0, total_rows, CHUNK):
            m = m_scr[r : r + CHUNK]
            s = s_scr[t, r : r + CHUNK]
            parts = [
                jnp.exp2((s[:, u : u + width] - m) * (scale * log2e))
                for u in range(0, s.shape[1], width)
            ]
            l_scr[r : r + CHUNK] += functools.reduce(jnp.add, parts)
            weights = jnp.concatenate(parts, axis=1).astype(jnp.bfloat16)
            acc_scr[r : r + CHUNK] += jnp.dot(
                weights, k_scr[...], preferred_element_type=jnp.float32
            )
        return carry

    lax.fori_loop(0, count, weigh, 0)
    row = lax.broadcasted_iota(jnp.int32, (rows, rows), 0)
    column = lax.broadcasted_iota(jnp.int32, (rows, rows), 1)
    halves = out_ref.shape[0]
    part = rows // halves
    none = count == 0
    for g in range(group):
        span = slice(g * rows, (g + 1) * rows)
        total = jnp.sum(l_scr[span], axis=1, keepdims=True)
        total = jnp.where(none, 1.0, total)
        out = (acc_scr[span] / total).astype(out_ref.dtype)
        for c in range(halves):
            out_ref[c, place_ref[g], 0] = out[c * part : (c + 1) * part]
        lse = jnp.where(none, EMPTY, m_scr[span] * scale + jnp.log(total))
        lse_ref[0, pl.ds(place_ref[g], 1), :] = jnp.sum(
            jnp.where(row == column, lse, 0.0), axis=0, keepdims=True
        )


def attend(slots, place, query, cosine, sine, keys, values, halves):
    prompts, rows, features = query.shape
    listed, width = cosine.shape[1:]
    group = features // width
    tokens = keys[0].shape[1]
    most = MOST * len(keys)
    part = rows // halves
    whole = pl.BlockSpec(memory_space=pltpu.VMEM)
    table = pl.BlockSpec((1, listed, width), lambda j, s, p: (j, 0, 0))
    return pl.pallas_call(
        functools.partial(attend_kernel, width**-0.5),
        out_shape=(
            jax.ShapeDtypeStruct((halves, group, prompts, part, width), jnp.bfloat16),
            jax.ShapeDtypeStruct((prompts, group, rows), jnp.float32),
        ),
        grid_spec=pltpu.PrefetchScalarGridSpec(
            num_scalar_prefetch=2,
            grid=(prompts,),
            in_specs=[pl.BlockSpec((1, rows, features), lambda j, s, p: (j, 0, 0)), table, table]
            + [whole] * 8,
            out_specs=(
                pl.BlockSpec((halves, group, 1, part, width), lambda j, s, p: (0, 0, j, 0, 0)),
                pl.BlockSpec((1, group, rows), lambda j, s, p: (j, 0, 0)),
            ),
            scratch_shapes=[
                pltpu.VMEM((rows * group, width), jnp.bfloat16),
                pltpu.VMEM((tokens, width), jnp.bfloat16),
                pltpu.VMEM((most, rows * group, tokens), jnp.float32),
                pltpu.VMEM((rows * group, width), jnp.float32),
                pltpu.VMEM((rows * group, width), jnp.float32),
                pltpu.VMEM((rows * group, width), jnp.float32),
                pltpu.SMEM((most,), jnp.int32),
            ],
        ),
        compiler_params=pltpu.CompilerParams(vmem_limit_bytes=48 * 1024 * 1024),
    )(slots, place, query, cosine, sine, *keys, *values)


def project_kernel(columns, where_ref, *refs):
    pieces, weight_ref, out_ref = refs[:columns], refs[columns], refs[columns + 1]
    heads, rows = pieces[0].shape[:2]
    left = jnp.concatenate(
        [jnp.concatenate([p[h] for h in range(heads)], axis=1) for p in pieces], axis=0
    )
    right = jnp.concatenate([weight_ref[h, 0] for h in range(heads)], axis=0)
    term = jnp.dot(left, right, preferred_element_type=jnp.float32).astype(out_ref.dtype)
    for d in range(columns):
        at = pl.multiple_of(where_ref[pl.num_programs(0) + d] * rows, rows)
        out_ref[0, pl.ds(at, rows), :] = term[d * rows : (d + 1) * rows]


def project(where, pieces, weight):
    columns = len(pieces)
    heads, rows, width = pieces[0].shape
    owners, out_columns = weight.shape[1], weight.shape[3]
    return pl.pallas_call(
        functools.partial(project_kernel, columns),
        out_shape=jax.ShapeDtypeStruct((owners, columns * rows, out_columns), jnp.bfloat16),
        grid_spec=pltpu.PrefetchScalarGridSpec(
            num_scalar_prefetch=1,
            grid=(owners,),
            in_specs=[pl.BlockSpec((heads, rows, width), lambda s, w: (0, 0, 0))] * columns
            + [pl.BlockSpec((heads, 1, width, out_columns), lambda s, w: (0, w[s], 0, 0))],
            out_specs=pl.BlockSpec((1, columns * rows, out_columns), lambda s, w: (s, 0, 0)),
        ),
        compiler_params=pltpu.CompilerParams(vmem_limit_bytes=32 * 1024 * 1024),
    )(where, *pieces, weight)


def merged(outs, lses):
    top = jnp.max(lses, axis=0)
    share = jnp.exp(lses - top)
    total = jnp.sum(share, axis=0)
    share = share / total
    out = jnp.sum(outs.astype(jnp.float32) * share[..., None], axis=0)
    return out, top + jnp.log(total)


def three_parts(value):
    first = lax.reduce_precision(value, 8, 7)
    rest = value - first
    second = lax.reduce_precision(rest, 8, 7)
    return jnp.stack([first, second, rest - second]).astype(jnp.bfloat16)


def body(
    queries, passage_keys, passage_values, offsets, out_weight, passage_list, targets, row_counts
):
    rows_of, columns = lax.axis_size(ROW), lax.axis_size(COL)
    y, x, c = lax.axis_index(ROW), lax.axis_index(COL), lax.axis_index("ctx")
    held, tokens, width = passage_keys.shape
    listed = passage_list.shape[1]
    prompt_rows, features = queries.shape[1:]
    group = features // width
    halves = lax.axis_size("ctx")
    half_rows = prompt_rows // halves

    keys = [passage_keys, shift(passage_keys, COL, -1), None, shift(passage_keys, COL, 1)]
    values = [passage_values, shift(passage_values, COL, -1), None, shift(passage_values, COL, 1)]
    keys[2] = shift(keys[3], COL, 1)
    values[2] = shift(values[1], COL, -1)

    asked = jnp.concatenate([passage_list, targets, row_counts[:, None]], axis=1)
    asked = lax.all_gather(asked, ROW, axis=0, tiled=True)
    near_offsets = jnp.concatenate(gather_pieces(offsets, COL))
    query = lax.all_gather(queries, ROW, axis=0, tiled=True)
    weight = out_weight.reshape(group, width, -1)
    weight = lax.all_to_all(weight, ROW, split_axis=0, concat_axis=0, tiled=True)
    weight = lax.all_gather(weight[None], "head", axis=0, tiled=True)

    near = columns * held
    local = asked[:, :listed] - y * near
    mine = (local >= 0) & (local < near)
    ahead = (local // held - x) % columns
    slots = jnp.where(mine, ahead * held + local % held, -1)
    same = slots[..., None] == jnp.arange(near, dtype=jnp.int32)
    delta = asked[:, listed : 2 * listed] - jnp.sum(
        jnp.where(same, near_offsets, 0), axis=-1
    )
    half = width // 2
    inverse = theta_base ** (-2.0 * jnp.arange(half, dtype=jnp.float32) / width)
    angle = delta.astype(jnp.float32)[..., None] * inverse
    cosine, sine = jnp.cos(angle), jnp.sin(angle)
    cosine = jnp.concatenate([cosine, cosine], axis=-1)
    sine = jnp.concatenate([-sine, sine], axis=-1)

    place = (jnp.arange(group, dtype=jnp.int32) - y) % rows_of
    out, lse = attend(slots.reshape(-1), place, query, cosine, sine, keys, values, halves)

    lse = jnp.transpose(lse.reshape(rows_of, group, halves, half_rows), (2, 1, 0, 3))
    swap = [(i, 1 - i) for i in range(2)]
    pick = functools.partial(lax.dynamic_index_in_dim, axis=0, keepdims=False)
    other = lax.ppermute(pick(out, 1 - c), "ctx", swap)
    other_lse = lax.ppermute(pick(lse, 1 - c), "ctx", swap)
    out, lse = merged(
        jnp.stack([pick(out, c), other]), jnp.stack([pick(lse, c), other_lse])
    )

    out = out.astype(jnp.bfloat16).reshape(group, rows_of * half_rows, width)
    parts = jnp.moveaxis(three_parts(lse), 0, 1).reshape(group, -1, width)
    extra = parts.shape[1]
    parts = jnp.pad(parts, ((0, 0), (0, -extra % 16), (0, 0)))
    got = jnp.stack(
        exchange([jnp.concatenate([out[d], parts[d]], axis=0) for d in range(rows_of)], ROW)
    )
    outs = got[:, : rows_of * half_rows].reshape(rows_of, rows_of, half_rows, width)
    lses = got[:, rows_of * half_rows : rows_of * half_rows + extra].astype(jnp.float32)
    lses = jnp.sum(lses.reshape(rows_of, 3, rows_of, half_rows), axis=1)
    attended, _ = merged(outs, lses)
    live = c * half_rows + jnp.arange(half_rows, dtype=jnp.int32) < asked[:, 2 * listed :]
    attended = jnp.where(live[..., None], attended, 0.0).astype(jnp.bfloat16)

    attended = lax.all_to_all(attended, "head", split_axis=0, concat_axis=0, tiled=True)
    where = jnp.concatenate(
        [
            (y + jnp.arange(rows_of, dtype=jnp.int32)) % rows_of,
            (x + jnp.arange(columns, dtype=jnp.int32)) % columns,
        ]
    )
    terms = project(where, gather_pieces(attended, COL), weight)
    terms = exchange([terms[d] for d in range(rows_of)], ROW)
    total = functools.reduce(jnp.add, [t.astype(jnp.float32) for t in terms])
    return total.astype(jnp.bfloat16)[None]


def solution(mesh):
    finer = Mesh(
        mesh.devices.reshape(8, 4, mesh.shape["ctx"], mesh.shape["head"]),
        ("lib_0", "lib_1", "ctx", "head"),
    )
    return jax.shard_map(
        body,
        mesh=finer,
        in_specs=(
            P(LIB, None, "head"),
            P(LIB, "ctx", "head"),
            P(LIB, "ctx", "head"),
            P(LIB),
            P("head", LIB),
            P(LIB, None),
            P(LIB, None),
            P(LIB),
        ),
        out_specs=P("ctx", "head", LIB),
        check_vma=False,
    )
```

```python
import functools

import jax
import jax.numpy as jnp
from jax import lax
from jax.experimental import pallas as pl
from jax.experimental.pallas import tpu as pltpu
from jax.sharding import Mesh
from jax.sharding import PartitionSpec as P

ROW, COL = "lib_0", "lib_1"
LIB = (ROW, COL)
theta_base = 500000.0
EMPTY = -1e30
CHUNK = 256
MOST = 2


def shift(value, axis, by):
    n = lax.axis_size(axis)
    return lax.ppermute(value, axis, [(i, (i + by) % n) for i in range(n)])


def far_first(n):
    return sorted(range(1, n), key=lambda d: -min(d, n - d))


def exchange(pieces, axis):
    arrived = list(pieces)
    for d in far_first(len(pieces)):
        arrived[d] = shift(pieces[d], axis, d)
    return arrived


def gather_pieces(value, axis):
    n = lax.axis_size(axis)
    pieces = [value] * n
    for d in far_first(n):
        pieces[d] = shift(value, axis, -d)
    return pieces


def attend_kernel(scale, pieces, first, last, slot_ref, place_ref, q_ref, cos_ref, sin_ref, *refs):
    key_refs, value_refs, refs = refs[:pieces], refs[pieces : 2 * pieces], refs[2 * pieces :]
    if not first:
        (before_ref, before_lse_ref), refs = refs[:2], refs[2:]
    out_ref, lse_ref, q_scr, tile, k_scr, s_scr, m_scr, l_scr, acc_scr, used, entry = refs
    prompt = pl.program_id(0)
    listed, width = cos_ref.shape[1:]
    rows = q_ref.shape[1]
    group = q_ref.shape[2] // width
    total_rows = rows * group
    held, tokens = key_refs[0].shape[:2]
    factor = scale * 1.4426950408889634
    row = lax.broadcasted_iota(jnp.int32, (rows, rows), 0)
    column = lax.broadcasted_iota(jnp.int32, (rows, rows), 1)
    chunks = [slice(r, r + CHUNK) for r in range(0, total_rows, CHUNK)]

    for g in range(group):
        span = slice(g * rows, (g + 1) * rows)
        q_scr[span] = q_ref[0, :, g * width : (g + 1) * width]
        if not first:
            lse = jnp.sum(
                jnp.where(row == column, before_lse_ref[0, g : g + 1, :], 0.0), axis=1, keepdims=True
            )
            lse = jnp.broadcast_to(lse * (1.0 / scale), (rows, width))
            m_scr[span] = lse
            l_scr[span] = lse
    if first:
        m_scr[...] = jnp.full_like(m_scr, EMPTY)

    def note(k, count):
        slot = slot_ref[prompt * listed + k]
        used[count] = slot
        entry[count] = k
        return count + jnp.where(slot >= 0, 1, 0)

    count = lax.fori_loop(0, listed, note, 0)
    pairs = (count + 1) // 2

    def fetch(refs, slot):
        if pieces == 1:
            return refs[0][slot]
        for d in range(pieces):

            @pl.when(slot // held == d)
            def _():
                tile[...] = refs[d][slot % held]

        return tile[...]

    def score(t, carry):
        for b in range(2):
            i = jnp.minimum(2 * t + b, count - 1)
            keys = fetch(key_refs, used[i]).astype(jnp.float32)
            cosine = cos_ref[0, pl.ds(entry[i], 1), :]
            sine = sin_ref[0, pl.ds(entry[i], 1), :]
            turned = keys * cosine + pltpu.roll(keys, width // 2, 1) * sine
            k_scr[b * tokens : (b + 1) * tokens] = turned.astype(jnp.bfloat16)
        both = 2 * t + 1 < count
        for span in chunks:
            s = lax.dot_general(
                q_scr[span],
                k_scr[...],
                (((1,), (1,)), ((), ())),
                preferred_element_type=jnp.float32,
            )
            highest = m_scr[span]
            for u in range(0, 2 * tokens, width):
                part = s[:, u : u + width]
                if u >= tokens:
                    part = jnp.where(both, part, EMPTY)
                s_scr[t, span, u : u + width] = part
                highest = jnp.maximum(highest, part)
            m_scr[span] = highest
        return carry

    lax.fori_loop(0, pairs, score, 0)
    lane = lax.broadcasted_iota(jnp.int32, (CHUNK, width), 1)
    for span in chunks:
        m = jnp.max(m_scr[span], axis=1, keepdims=True)
        m = jnp.broadcast_to(m, (CHUNK, width))
        m_scr[span] = m
        if first:
            l_scr[span] = jnp.zeros_like(m)
            acc_scr[span] = jnp.zeros_like(m)
        else:
            weight = jnp.exp2((l_scr[span] - m) * factor)
            l_scr[span] = jnp.where(lane == 0, weight, 0.0)
            acc_scr[span] = before_ref[0, span] * weight

    def weigh(t, carry):
        for b in range(2):
            i = jnp.minimum(2 * t + b, count - 1)
            k_scr[b * tokens : (b + 1) * tokens] = fetch(value_refs, used[i])
        for span in chunks:
            m = m_scr[span]
            parts = [
                jnp.exp2((s_scr[t, span, u : u + width] - m) * factor)
                for u in range(0, 2 * tokens, width)
            ]
            l_scr[span] += functools.reduce(jnp.add, parts)
            weights = jnp.concatenate([p.astype(jnp.bfloat16) for p in parts], axis=1)
            acc_scr[span] += jnp.dot(weights, k_scr[...], preferred_element_type=jnp.float32)
        return carry

    lax.fori_loop(0, pairs, weigh, 0)
    for g in range(group):
        span = slice(g * rows, (g + 1) * rows)
        total = jnp.sum(l_scr[span], axis=1, keepdims=True)
        if first:
            total = jnp.where(count == 0, 1.0, total)
        out = acc_scr[span] * (1.0 / total)
        lse = m_scr[span] * scale + jnp.log(total)
        lse = jnp.sum(jnp.where(row == column, lse, 0.0), axis=0, keepdims=True)
        if last:
            halves = out_ref.shape[0]
            part = rows // halves
            for c in range(halves):
                out_ref[c, place_ref[g], 0] = out[c * part : (c + 1) * part].astype(out_ref.dtype)
            lse_ref[0, pl.ds(place_ref[g], 1), :] = lse
        else:
            out_ref[0, span] = out
            lse_ref[0, g : g + 1, :] = lse


def attend(slots, place, query, cosine, sine, keys, values, before, halves):
    prompts, rows, features = query.shape
    listed, width = cosine.shape[1:]
    group = features // width
    tokens = keys[0].shape[1]
    most = MOST * len(keys)
    whole = pl.BlockSpec(memory_space=pltpu.VMEM)
    table = pl.BlockSpec((1, listed, width), lambda j, s, p: (j, 0, 0))
    state = [
        pl.BlockSpec((1, rows * group, width), lambda j, s, p: (j, 0, 0)),
        pl.BlockSpec((1, group, rows), lambda j, s, p: (j, 0, 0)),
    ]
    if halves:
        part = rows // halves
        out = jax.ShapeDtypeStruct((halves, group, prompts, part, width), jnp.bfloat16)
        out_spec = pl.BlockSpec((halves, group, 1, part, width), lambda j, s, p: (0, 0, j, 0, 0))
    else:
        out = jax.ShapeDtypeStruct((prompts, rows * group, width), jnp.float32)
        out_spec = state[0]
    work = prompts * most // 2 * rows * group * tokens
    return pl.pallas_call(
        functools.partial(attend_kernel, width**-0.5, len(keys), before is None, bool(halves)),
        out_shape=(out, jax.ShapeDtypeStruct((prompts, group, rows), jnp.float32)),
        grid_spec=pltpu.PrefetchScalarGridSpec(
            num_scalar_prefetch=2,
            grid=(prompts,),
            in_specs=[pl.BlockSpec((1, rows, features), lambda j, s, p: (j, 0, 0)), table, table]
            + [whole] * (2 * len(keys))
            + (state if before else []),
            out_specs=(out_spec, state[1]),
            scratch_shapes=[
                pltpu.VMEM((rows * group, width), jnp.bfloat16),
                pltpu.VMEM((tokens, width), jnp.bfloat16),
                pltpu.VMEM((2 * tokens, width), jnp.bfloat16),
                pltpu.VMEM((most // 2, rows * group, 2 * tokens), jnp.float32),
                pltpu.VMEM((rows * group, width), jnp.float32),
                pltpu.VMEM((rows * group, width), jnp.float32),
                pltpu.VMEM((rows * group, width), jnp.float32),
                pltpu.SMEM((most + 1,), jnp.int32),
                pltpu.SMEM((most + 1,), jnp.int32),
            ],
        ),
        cost_estimate=pl.CostEstimate(
            flops=4 * work * width, bytes_accessed=8 * work, transcendentals=work
        ),
        compiler_params=pltpu.CompilerParams(vmem_limit_bytes=48 * 1024 * 1024),
    )(slots, place, query, cosine, sine, *keys, *values, *(before or ()))


def project_kernel(columns, where_ref, *refs):
    pieces, weight_ref, out_ref = refs[:columns], refs[columns], refs[columns + 1]
    heads, rows = pieces[0].shape[:2]
    left = jnp.concatenate(
        [jnp.concatenate([p[h] for h in range(heads)], axis=1) for p in pieces], axis=0
    )
    right = jnp.concatenate([weight_ref[h, 0] for h in range(heads)], axis=0)
    term = jnp.dot(left, right, preferred_element_type=jnp.float32).astype(out_ref.dtype)
    for d in range(columns):
        at = pl.multiple_of(where_ref[pl.num_programs(0) + d] * rows, rows)
        out_ref[0, pl.ds(at, rows), :] = term[d * rows : (d + 1) * rows]


def project(where, pieces, weight):
    columns = len(pieces)
    heads, rows, width = pieces[0].shape
    owners, out_columns = weight.shape[1], weight.shape[3]
    return pl.pallas_call(
        functools.partial(project_kernel, columns),
        out_shape=jax.ShapeDtypeStruct((owners, columns * rows, out_columns), jnp.bfloat16),
        grid_spec=pltpu.PrefetchScalarGridSpec(
            num_scalar_prefetch=1,
            grid=(owners,),
            in_specs=[pl.BlockSpec((heads, rows, width), lambda s, w: (0, 0, 0))] * columns
            + [pl.BlockSpec((heads, 1, width, out_columns), lambda s, w: (0, w[s], 0, 0))],
            out_specs=pl.BlockSpec((1, columns * rows, out_columns), lambda s, w: (s, 0, 0)),
        ),
        compiler_params=pltpu.CompilerParams(vmem_limit_bytes=32 * 1024 * 1024),
    )(where, *pieces, weight)


def merged(outs, lses):
    top = jnp.max(lses, axis=0)
    share = jnp.exp(lses - top)
    total = jnp.sum(share, axis=0)
    share = share / total
    out = jnp.sum(outs.astype(jnp.float32) * share[..., None], axis=0)
    return out, top + jnp.log(total)


def three_parts(value):
    first = lax.reduce_precision(value, 8, 7)
    rest = value - first
    second = lax.reduce_precision(rest, 8, 7)
    return jnp.stack([first, second, rest - second]).astype(jnp.bfloat16)


def body(
    queries, passage_keys, passage_values, offsets, out_weight, passage_list, targets, row_counts
):
    rows_of, columns = lax.axis_size(ROW), lax.axis_size(COL)
    y, x, c = lax.axis_index(ROW), lax.axis_index(COL), lax.axis_index("ctx")
    held, tokens, width = passage_keys.shape
    listed = passage_list.shape[1]
    prompt_rows, features = queries.shape[1:]
    group = features // width
    halves = lax.axis_size("ctx")
    half_rows = prompt_rows // halves

    near_offsets = gather_pieces(offsets, COL)
    own_keys, own_values, near_offsets = lax.optimization_barrier(
        (passage_keys, passage_values, near_offsets)
    )
    keys = [own_keys, shift(own_keys, COL, -1), None, shift(own_keys, COL, 1)]
    values = [own_values, shift(own_values, COL, -1), None, shift(own_values, COL, 1)]
    keys[2] = shift(keys[3], COL, 1)
    values[2] = shift(values[1], COL, -1)

    asked = jnp.concatenate([passage_list, targets, row_counts[:, None]], axis=1)
    asked = lax.all_gather(asked, ROW, axis=0, tiled=True)
    query = lax.all_gather(queries, ROW, axis=0, tiled=True)
    weight = out_weight.reshape(group, width, -1)
    weight = lax.all_to_all(weight, ROW, split_axis=0, concat_axis=0, tiled=True)
    weight = lax.all_gather(weight[None], "head", axis=0, tiled=True)

    near = columns * held
    local = asked[:, :listed] - y * near
    mine = (local >= 0) & (local < near)
    ahead = (local // held - x) % columns
    within = local % held
    slots = jnp.where(mine, ahead * held + within, -1)
    same = slots[..., None] == jnp.arange(near, dtype=jnp.int32)
    delta = asked[:, listed : 2 * listed] - jnp.sum(
        jnp.where(same, jnp.concatenate(near_offsets), 0), axis=-1
    )
    half = width // 2
    inverse = theta_base ** (-2.0 * jnp.arange(half, dtype=jnp.float32) / width)
    angle = delta.astype(jnp.float32)[..., None] * inverse
    cosine, sine = jnp.cos(angle), jnp.sin(angle)
    cosine = jnp.concatenate([cosine, cosine], axis=-1)
    sine = jnp.concatenate([-sine, sine], axis=-1)

    place = (jnp.arange(group, dtype=jnp.int32) - y) % rows_of
    early = (0, 1, 3)
    soon = jnp.where(mine & (ahead != 2), jnp.where(ahead == 3, 2, ahead) * held + within, -1)
    late = jnp.where(mine & (ahead == 2), within, -1)
    before = attend(
        soon.reshape(-1), place, query, cosine, sine,
        [keys[d] for d in early], [values[d] for d in early], None, 0,
    )
    out, lse = attend(
        late.reshape(-1), place, query, cosine, sine, keys[2:3], values[2:3], before, halves
    )

    lse = jnp.transpose(lse.reshape(rows_of, group, halves, half_rows), (2, 1, 0, 3))
    swap = [(i, 1 - i) for i in range(2)]
    pick = functools.partial(lax.dynamic_index_in_dim, axis=0, keepdims=False)
    other = lax.ppermute(pick(out, 1 - c), "ctx", swap)
    other_lse = lax.ppermute(pick(lse, 1 - c), "ctx", swap)
    out, lse = merged(
        jnp.stack([pick(out, c), other]), jnp.stack([pick(lse, c), other_lse])
    )

    out = out.astype(jnp.bfloat16).reshape(group, rows_of * half_rows, width)
    parts = jnp.moveaxis(three_parts(lse), 0, 1).reshape(group, -1, width)
    extra = parts.shape[1]
    parts = jnp.pad(parts, ((0, 0), (0, -extra % 16), (0, 0)))
    got = jnp.stack(
        exchange([jnp.concatenate([out[d], parts[d]], axis=0) for d in range(rows_of)], ROW)
    )
    outs = got[:, : rows_of * half_rows].reshape(rows_of, rows_of, half_rows, width)
    lses = got[:, rows_of * half_rows : rows_of * half_rows + extra].astype(jnp.float32)
    lses = jnp.sum(lses.reshape(rows_of, 3, rows_of, half_rows), axis=1)
    attended, _ = merged(outs, lses)
    live = c * half_rows + jnp.arange(half_rows, dtype=jnp.int32) < asked[:, 2 * listed :]
    attended = jnp.where(live[..., None], attended, 0.0).astype(jnp.bfloat16)

    attended = lax.all_to_all(attended, "head", split_axis=0, concat_axis=0, tiled=True)
    where = jnp.concatenate(
        [
            (y + jnp.arange(rows_of, dtype=jnp.int32)) % rows_of,
            (x + jnp.arange(columns, dtype=jnp.int32)) % columns,
        ]
    )
    terms = project(where, gather_pieces(attended, COL), weight)
    terms = exchange([terms[d] for d in range(rows_of)], ROW)
    total = functools.reduce(jnp.add, [t.astype(jnp.float32) for t in terms])
    return total.astype(jnp.bfloat16)[None]


def solution(mesh):
    finer = Mesh(
        mesh.devices.reshape(8, 4, mesh.shape["ctx"], mesh.shape["head"]),
        ("lib_0", "lib_1", "ctx", "head"),
    )
    return jax.shard_map(
        body,
        mesh=finer,
        in_specs=(
            P(LIB, None, "head"),
            P(LIB, "ctx", "head"),
            P(LIB, "ctx", "head"),
            P(LIB),
            P("head", LIB),
            P(LIB, None),
            P(LIB, None),
            P(LIB),
        ),
        out_specs=P("ctx", "head", LIB),
        check_vma=False,
    )
```

```python
import functools

import jax
import jax.numpy as jnp
from jax import lax
from jax.experimental import pallas as pl
from jax.experimental.pallas import tpu as pltpu
from jax.sharding import Mesh
from jax.sharding import PartitionSpec as P

ROW, COL = "lib_0", "lib_1"
LIB = (ROW, COL)
theta_base = 500000.0
EMPTY = -1e30
CHUNK = 256
MOST = 2


def shift(value, axis, by):
    n = lax.axis_size(axis)
    return lax.ppermute(value, axis, [(i, (i + by) % n) for i in range(n)])


def far_first(n):
    return sorted(range(1, n), key=lambda d: -min(d, n - d))


def coded(integers):
    return (integers // 128).astype(jnp.bfloat16), (integers % 128).astype(jnp.bfloat16)


def decoded(high, low):
    return high.astype(jnp.int32) * 128 + low.astype(jnp.int32)


def gather_pieces(value, axis):
    n = lax.axis_size(axis)
    pieces = [value] * n
    for d in far_first(n):
        pieces[d] = shift(value, axis, -d)
    return pieces


def attend_kernel(scale, pieces, first, last, slot_ref, q_ref, cos_ref, sin_ref, *refs):
    key_refs, value_refs, refs = refs[:pieces], refs[pieces : 2 * pieces], refs[2 * pieces :]
    if not first:
        (before_ref, before_lse_ref), refs = refs[:2], refs[2:]
    out_ref, lse_ref, q_scr, tile, k_scr, v_scr, s_scr, m_scr, acc_scr, used, entry = refs
    prompt = pl.program_id(0)
    listed, width = cos_ref.shape[1:]
    rows = q_ref.shape[1]
    group = q_ref.shape[2] // width
    total_rows = rows * group
    tokens = tile.shape[0]
    held = key_refs[0].shape[0] // tokens
    factor = scale * 1.4426950408889634
    chunks = [slice(r, r + CHUNK) for r in range(0, total_rows, CHUNK)]

    @pl.when(prompt == 0)
    def _():
        v_scr[:, width:] = jnp.ones((2 * tokens, width), v_scr.dtype)

    for g in range(group):
        q_scr[g * rows : (g + 1) * rows] = q_ref[0, :, g * width : (g + 1) * width]
    for span in chunks:
        if first:
            m_scr[span] = jnp.full((CHUNK, width), EMPTY, jnp.float32)
        else:
            m_scr[span] = before_lse_ref[0, span] * (1.0 / scale)

    def note(k, count):
        slot = slot_ref[prompt * listed + k]
        used[count] = slot
        entry[count] = k
        return count + jnp.where(slot >= 0, 1, 0)

    count = lax.fori_loop(0, listed, note, 0)
    pairs = (count + 1) // 2

    def fetch(refs, slot):
        def at(index):
            return pl.ds(pl.multiple_of(index * tokens, tokens), tokens)

        if pieces == 1:
            return refs[0][at(slot)]
        for d in range(pieces):

            @pl.when(slot // held == d)
            def _():
                tile[...] = refs[d][at(slot % held)]

        return tile[...]

    def score(t, carry):
        for b in range(2):
            i = jnp.minimum(2 * t + b, count - 1)
            keys = fetch(key_refs, used[i]).astype(jnp.float32)
            cosine = cos_ref[0, pl.ds(entry[i], 1), :]
            sine = sin_ref[0, pl.ds(entry[i], 1), :]
            turned = keys * cosine + pltpu.roll(keys, width // 2, 1) * sine
            k_scr[b * tokens : (b + 1) * tokens] = turned.astype(jnp.bfloat16)
        both = 2 * t + 1 < count
        for span in chunks:
            s = lax.dot_general(
                q_scr[span],
                k_scr[...],
                (((1,), (1,)), ((), ())),
                preferred_element_type=jnp.float32,
            )
            highest = m_scr[span]
            for u in range(0, 2 * tokens, width):
                part = s[:, u : u + width]
                if u >= tokens:
                    part = jnp.where(both, part, EMPTY)
                s_scr[t, span, u : u + width] = part
                highest = jnp.maximum(highest, part)
            m_scr[span] = highest
        return carry

    lax.fori_loop(0, pairs, score, 0)
    for span in chunks:
        m = jnp.broadcast_to(jnp.max(m_scr[span], axis=1, keepdims=True), (CHUNK, width))
        m_scr[span] = m
        if first:
            acc_scr[span] = jnp.zeros((CHUNK, 2 * width), jnp.float32)
        else:
            weight = jnp.exp2((before_lse_ref[0, span] * (1.0 / scale) - m) * factor)
            acc_scr[span, :width] = before_ref[0, span] * weight
            acc_scr[span, width:] = weight

    def weigh(t, carry):
        for b in range(2):
            i = jnp.minimum(2 * t + b, count - 1)
            v_scr[b * tokens : (b + 1) * tokens, :width] = fetch(value_refs, used[i])
        for span in chunks:
            m = m_scr[span]
            parts = [
                jnp.exp2((s_scr[t, span, u : u + width] - m) * factor)
                for u in range(0, 2 * tokens, width)
            ]
            weights = jnp.concatenate([p.astype(jnp.bfloat16) for p in parts], axis=1)
            acc_scr[span] += jnp.dot(weights, v_scr[...], preferred_element_type=jnp.float32)
        return carry

    lax.fori_loop(0, pairs, weigh, 0)
    row = lax.broadcasted_iota(jnp.int32, (rows, rows), 0)
    column = lax.broadcasted_iota(jnp.int32, (rows, rows), 1)
    for g in range(group):
        span = slice(g * rows, (g + 1) * rows)
        total = acc_scr[span, width:]
        if first:
            total = jnp.where(count == 0, 1.0, total)
        out = acc_scr[span, :width] / total
        lse = m_scr[span] * scale + jnp.log(total)
        if last:
            halves = out_ref.shape[0]
            part = rows // halves
            for c in range(halves):
                out_ref[c, g, 0] = out[c * part : (c + 1) * part].astype(out_ref.dtype)
            lse_ref[0, g : g + 1, :] = jnp.sum(
                jnp.where(row == column, lse, 0.0), axis=0, keepdims=True
            )
        else:
            out_ref[0, span] = out
            lse_ref[0, span] = lse


def attend(slots, query, cosine, sine, keys, values, before, halves, rows, tokens):
    prompts, _, features = query.shape
    listed, width = cosine.shape[1:]
    group = features // width
    most = MOST * len(keys)
    whole = pl.BlockSpec(memory_space=pltpu.VMEM)
    table = pl.BlockSpec((1, listed, width), lambda j, s: (j, 0, 0))
    state = pl.BlockSpec((1, rows * group, width), lambda j, s: (j, 0, 0))
    if halves:
        part = rows // halves
        out = (
            jax.ShapeDtypeStruct((halves, group, prompts, part, width), jnp.bfloat16),
            jax.ShapeDtypeStruct((prompts, group, rows), jnp.float32),
        )
        out_specs = (
            pl.BlockSpec((halves, group, 1, part, width), lambda j, s: (0, 0, j, 0, 0)),
            pl.BlockSpec((1, group, rows), lambda j, s: (j, 0, 0)),
        )
    else:
        out = (jax.ShapeDtypeStruct((prompts, rows * group, width), jnp.float32),) * 2
        out_specs = (state, state)
    work = prompts * most // 2 * rows * group * tokens
    return pl.pallas_call(
        functools.partial(attend_kernel, width**-0.5, len(keys), before is None, bool(halves)),
        out_shape=out,
        grid_spec=pltpu.PrefetchScalarGridSpec(
            num_scalar_prefetch=1,
            grid=(prompts,),
            in_specs=[pl.BlockSpec((1, rows, features), lambda j, s: (j, 0, 0)), table, table]
            + [whole] * (2 * len(keys))
            + ([state, state] if before else []),
            out_specs=out_specs,
            scratch_shapes=[
                pltpu.VMEM((rows * group, width), jnp.bfloat16),
                pltpu.VMEM((tokens, width), jnp.bfloat16),
                pltpu.VMEM((2 * tokens, width), jnp.bfloat16),
                pltpu.VMEM((2 * tokens, 2 * width), jnp.bfloat16),
                pltpu.VMEM((most // 2, rows * group, 2 * tokens), jnp.float32),
                pltpu.VMEM((rows * group, width), jnp.float32),
                pltpu.VMEM((rows * group, 2 * width), jnp.float32),
                pltpu.SMEM((most + 1,), jnp.int32),
                pltpu.SMEM((most + 1,), jnp.int32),
            ],
        ),
        cost_estimate=pl.CostEstimate(
            flops=4 * work * width, bytes_accessed=8 * work, transcendentals=work
        ),
        compiler_params=pltpu.CompilerParams(vmem_limit_bytes=48 * 1024 * 1024),
    )(slots, query, cosine, sine, *keys, *values, *(before or ()))


def project_kernel(columns, where_ref, *refs):
    pieces, weight_ref, out_ref = refs[:columns], refs[columns], refs[columns + 1]
    heads, rows = pieces[0].shape[:2]
    left = jnp.concatenate(
        [jnp.concatenate([p[h] for h in range(heads)], axis=1) for p in pieces], axis=0
    )
    right = jnp.concatenate([weight_ref[h, 0] for h in range(heads)], axis=0)
    term = jnp.dot(left, right, preferred_element_type=jnp.float32).astype(out_ref.dtype)
    for d in range(columns):
        at = pl.multiple_of(where_ref[d] * rows, rows)
        out_ref[0, pl.ds(at, rows), :] = term[d * rows : (d + 1) * rows]


def project(where, pieces, weight):
    columns = len(pieces)
    heads, rows, width = pieces[0].shape
    owners, out_columns = weight.shape[1], weight.shape[3]
    return pl.pallas_call(
        functools.partial(project_kernel, columns),
        out_shape=jax.ShapeDtypeStruct((owners, columns * rows, out_columns), jnp.bfloat16),
        grid_spec=pltpu.PrefetchScalarGridSpec(
            num_scalar_prefetch=1,
            grid=(owners,),
            in_specs=[pl.BlockSpec((heads, rows, width), lambda s, w: (0, 0, 0))] * columns
            + [pl.BlockSpec((heads, 1, width, out_columns), lambda s, w: (0, s, 0, 0))],
            out_specs=pl.BlockSpec((1, columns * rows, out_columns), lambda s, w: (s, 0, 0)),
        ),
        compiler_params=pltpu.CompilerParams(vmem_limit_bytes=32 * 1024 * 1024),
    )(where, *pieces, weight)


def merged(outs, lses):
    top = jnp.max(lses, axis=0)
    share = jnp.exp(lses - top)
    total = jnp.sum(share, axis=0)
    share = share / total
    out = jnp.sum(outs.astype(jnp.float32) * share[..., None], axis=0)
    return out, top + jnp.log(total)


def three_parts(value):
    first = lax.reduce_precision(value, 8, 7)
    rest = value - first
    second = lax.reduce_precision(rest, 8, 7)
    return jnp.stack([first, second, rest - second]).astype(jnp.bfloat16)


def turns(delta, width):
    half = width // 2
    inverse = theta_base ** (-2.0 * jnp.arange(half, dtype=jnp.float32) / width)
    angle = delta.astype(jnp.float32)[..., None] * inverse
    cosine, sine = jnp.cos(angle), jnp.sin(angle)
    return jnp.concatenate([cosine, cosine], axis=-1), jnp.concatenate([-sine, sine], axis=-1)


def body(
    queries, passage_keys, passage_values, offsets, out_weight, passage_list, targets, row_counts
):
    rows_of, columns = lax.axis_size(ROW), lax.axis_size(COL)
    y, x, c = lax.axis_index(ROW), lax.axis_index(COL), lax.axis_index("ctx")
    z = lax.axis_index("head")
    held, tokens, width = passage_keys.shape
    listed = passage_list.shape[1]
    prompt_rows, features = queries.shape[1:]
    group = features // width
    halves = lax.axis_size("ctx")
    half_rows = prompt_rows // halves

    behind = jnp.pad(jnp.stack(coded(offsets)), ((0, 14), (0, width - held)))
    own_keys = jnp.concatenate([passage_keys.reshape(-1, width), behind], axis=0)
    own_values = passage_values.reshape(-1, width)
    keys = [own_keys, shift(own_keys, COL, -1), None, shift(own_keys, COL, 1)]
    values = [own_values, shift(own_values, COL, -1), None, shift(own_values, COL, 1)]
    keys[2] = shift(keys[3], COL, 1)
    values[2] = shift(values[1], COL, -1)

    asked = jnp.concatenate([passage_list[0], targets[0], row_counts])
    asked = jnp.stack(coded(asked))
    asked = jnp.pad(asked, ((0, 14), (0, features - asked.shape[1])))
    query = jnp.concatenate([queries, asked[None]], axis=1)
    query = lax.all_gather(query, ROW, axis=0, tiled=True)
    asked = decoded(query[:, prompt_rows], query[:, prompt_rows + 1])
    weight = out_weight.reshape(group, width, -1)
    weight = lax.all_to_all(weight, ROW, split_axis=0, concat_axis=0, tiled=True)
    weight = lax.all_gather(weight[None], "head", axis=0, tiled=True)

    local = asked[:, :listed] - y * columns * held
    mine = (local >= 0) & (local < columns * held)
    ahead = (local // held - x) % columns
    within = local % held

    def tables(order, pieces):
        slots = jnp.full_like(within, -1)
        for at, d in enumerate(order):
            slots = jnp.where(mine & (ahead == d), at * held + within, slots)
        tails = jnp.stack([p[held * tokens : held * tokens + 2, :held] for p in pieces])
        near = decoded(tails[:, 0], tails[:, 1]).reshape(-1)
        same = slots[..., None] == jnp.arange(len(order) * held, dtype=jnp.int32)
        moved = asked[:, listed : 2 * listed] - jnp.sum(jnp.where(same, near, 0), axis=-1)
        return (slots.reshape(-1), *turns(moved, width))

    before = None
    for order, laid_out in (((0, 1, 3), 0), ((2,), halves)):
        pieces = [keys[d] for d in order]
        if before is not None:
            before, pieces = lax.optimization_barrier((before, pieces))
        slots, cosine, sine = tables(order, pieces)
        before = attend(
            slots, query, cosine, sine, pieces, [values[d] for d in order], before, laid_out,
            prompt_rows, tokens,
        )
    out, lse = before

    lse = jnp.transpose(lse.reshape(rows_of, group, halves, half_rows), (2, 1, 0, 3))
    swap = [(i, 1 - i) for i in range(2)]
    pick = functools.partial(lax.dynamic_index_in_dim, axis=0, keepdims=False)
    other = lax.ppermute(pick(out, 1 - c), "ctx", swap)
    other_lse = lax.ppermute(pick(lse, 1 - c), "ctx", swap)
    out, lse = merged(
        jnp.stack([pick(out, c), other]), jnp.stack([pick(lse, c), other_lse])
    )

    out = out.astype(jnp.bfloat16).reshape(group * rows_of, half_rows, width)
    parts = jnp.moveaxis(three_parts(lse.reshape(group * rows_of, half_rows)), 0, 1)
    parts = jnp.pad(parts, ((0, 0), (0, 5), (0, width - half_rows)))
    sent = jnp.concatenate([out, parts], axis=1)
    got = lax.all_to_all(sent, (ROW, "head"), split_axis=0, concat_axis=0, tiled=True)
    got = got.reshape(rows_of, -1, half_rows + 8, width)
    lses = got[:, :, half_rows : half_rows + 3, :half_rows].astype(jnp.float32)
    attended, _ = merged(got[:, :, :half_rows], jnp.sum(lses, axis=2))
    count = lax.dynamic_index_in_dim(asked[:, 2 * listed], z, keepdims=False)
    live = c * half_rows + jnp.arange(half_rows, dtype=jnp.int32) < count
    attended = jnp.where(live[:, None], attended, 0.0).astype(jnp.bfloat16)

    where = (x + jnp.arange(columns, dtype=jnp.int32)) % columns
    terms = project(where, gather_pieces(attended, COL), weight)
    terms = lax.all_to_all(terms, ROW, split_axis=0, concat_axis=0, tiled=True)
    total = jnp.sum(terms.astype(jnp.float32), axis=0)
    return total.astype(jnp.bfloat16)[None]


def solution(mesh):
    finer = Mesh(
        mesh.devices.reshape(8, 4, mesh.shape["ctx"], mesh.shape["head"]),
        ("lib_0", "lib_1", "ctx", "head"),
    )
    return jax.shard_map(
        body,
        mesh=finer,
        in_specs=(
            P(LIB, None, "head"),
            P(LIB, "ctx", "head"),
            P(LIB, "ctx", "head"),
            P(LIB),
            P("head", LIB),
            P(LIB, None),
            P(LIB, None),
            P(LIB),
        ),
        out_specs=P("ctx", "head", LIB),
        check_vma=False,
    )
```

```python
import functools

import jax
import jax.numpy as jnp
from jax import lax
from jax.experimental import pallas as pl
from jax.experimental.pallas import tpu as pltpu
from jax.sharding import Mesh
from jax.sharding import PartitionSpec as P

ROW, COL = "lib_0", "lib_1"
LIB = (ROW, COL)
theta_base = 500000.0
EMPTY = -1e30
CHUNK = 256
MOST = 2


def shift(value, axis, by):
    n = lax.axis_size(axis)
    return lax.ppermute(value, axis, [(i, (i + by) % n) for i in range(n)])


def coded(integers):
    return (integers // 128).astype(jnp.bfloat16), (integers % 128).astype(jnp.bfloat16)


def decoded(high, low):
    return high.astype(jnp.int32) * 128 + low.astype(jnp.int32)


def attend_kernel(scale, pieces, first, last, values_at, slot_ref, q_ref, cos_ref, sin_ref, *refs):
    key_refs, refs = refs[:pieces], refs[pieces:]
    value_refs = key_refs
    if last:
        value_refs, refs = refs[:pieces], refs[pieces:]
    if not first:
        (before_ref, before_lse_ref), refs = refs[:2], refs[2:]
    if last:
        other_ref, refs = refs[1], refs[:1] + refs[2:]
    out_ref, lse_ref, q_scr, tile, k_scr, v_scr, s_scr, m_scr, acc_scr, used, entry = refs
    prompt = pl.program_id(0)
    listed, width = cos_ref.shape[1:]
    rows = q_ref.shape[1]
    group = q_ref.shape[2] // width
    total_rows = rows * group
    tokens = tile.shape[0]
    held = key_refs[0].shape[0] // tokens if last else values_at // tokens
    factor = scale * 1.4426950408889634
    chunks = [slice(r, r + CHUNK) for r in range(0, total_rows, CHUNK)]

    @pl.when(prompt == 0)
    def _():
        v_scr[:, width:] = jnp.ones((2 * tokens, width), v_scr.dtype)

    for g in range(group):
        q_scr[g * rows : (g + 1) * rows] = q_ref[0, :, g * width : (g + 1) * width]
    for span in chunks:
        if first:
            m_scr[span] = jnp.full((CHUNK, width), EMPTY, jnp.float32)
        else:
            m_scr[span] = before_lse_ref[0, span] * (1.0 / scale)

    def note(k, count):
        slot = slot_ref[prompt * listed + k]
        used[count] = slot
        entry[count] = k
        return count + jnp.where(slot >= 0, 1, 0)

    count = lax.fori_loop(0, listed, note, 0)
    pairs = (count + 1) // 2

    def fetch(refs, slot, start):
        def at(index):
            return pl.ds(pl.multiple_of(index * tokens + start, 16), tokens)

        if pieces == 1:
            return refs[0][at(slot)]
        for d in range(pieces):

            @pl.when(slot // held == d)
            def _():
                tile[...] = refs[d][at(slot % held)]

        return tile[...]

    def score(t, carry):
        for b in range(2):
            i = jnp.minimum(2 * t + b, count - 1)
            keys = fetch(key_refs, used[i], 0).astype(jnp.float32)
            cosine = cos_ref[0, pl.ds(entry[i], 1), :]
            sine = sin_ref[0, pl.ds(entry[i], 1), :]
            turned = keys * cosine + pltpu.roll(keys, width // 2, 1) * sine
            k_scr[b * tokens : (b + 1) * tokens] = turned.astype(jnp.bfloat16)
        both = 2 * t + 1 < count
        for span in chunks:
            s = lax.dot_general(
                q_scr[span],
                k_scr[...],
                (((1,), (1,)), ((), ())),
                preferred_element_type=jnp.float32,
            )
            highest = m_scr[span]
            for u in range(0, 2 * tokens, width):
                part = s[:, u : u + width]
                if u >= tokens:
                    part = jnp.where(both, part, EMPTY)
                s_scr[t, span, u : u + width] = part
                highest = jnp.maximum(highest, part)
            m_scr[span] = highest
        return carry

    lax.fori_loop(0, pairs, score, 0)
    for span in chunks:
        m = jnp.broadcast_to(jnp.max(m_scr[span], axis=1, keepdims=True), (CHUNK, width))
        m_scr[span] = m
        if first:
            acc_scr[span] = jnp.zeros((CHUNK, 2 * width), jnp.float32)
        else:
            weight = jnp.exp2((before_lse_ref[0, span] * (1.0 / scale) - m) * factor)
            acc_scr[span, :width] = before_ref[0, span] * weight
            acc_scr[span, width:] = weight

    def weigh(t, carry):
        for b in range(2):
            i = jnp.minimum(2 * t + b, count - 1)
            v_scr[b * tokens : (b + 1) * tokens, :width] = fetch(value_refs, used[i], 0 if last else values_at)
        for span in chunks:
            m = m_scr[span]
            parts = [
                jnp.exp2((s_scr[t, span, u : u + width] - m) * factor)
                for u in range(0, 2 * tokens, width)
            ]
            weights = jnp.concatenate([p.astype(jnp.bfloat16) for p in parts], axis=1)
            acc_scr[span] += jnp.dot(weights, v_scr[...], preferred_element_type=jnp.float32)
        return carry

    lax.fori_loop(0, pairs, weigh, 0)
    if last:
        core = slot_ref[pl.num_programs(0) * listed]
    row = lax.broadcasted_iota(jnp.int32, (rows, rows), 0)
    column = lax.broadcasted_iota(jnp.int32, (rows, rows), 1)
    for g in range(group):
        span = slice(g * rows, (g + 1) * rows)
        total = acc_scr[span, width:]
        if first:
            total = jnp.where(count == 0, 1.0, total)
        out = acc_scr[span, :width] / total
        lse = m_scr[span] * scale + jnp.log(total)
        if last:
            out = out.astype(out_ref.dtype)
            part = rows // 2
            for c in range(2):

                @pl.when(core == c)
                def _():
                    out_ref[g, 0] = out[c * part : (c + 1) * part]
                    other_ref[g, 0] = out[(1 - c) * part : (2 - c) * part]

            lse_ref[0, g : g + 1, :] = jnp.sum(
                jnp.where(row == column, lse, 0.0), axis=0, keepdims=True
            )
        else:
            out_ref[0, span] = out
            lse_ref[0, span] = lse


def attend(slots, query, cosine, sine, keys, values, before, rows, tokens, values_at):
    prompts, _, features = query.shape
    listed, width = cosine.shape[1:]
    group = features // width
    most = MOST * len(keys)
    whole = pl.BlockSpec(memory_space=pltpu.VMEM)
    table = pl.BlockSpec((1, listed, width), lambda j, s: (j, 0, 0))
    state = pl.BlockSpec((1, rows * group, width), lambda j, s: (j, 0, 0))
    if before:
        half = jax.ShapeDtypeStruct((group, prompts, rows // 2, width), jnp.bfloat16)
        half_spec = pl.BlockSpec((group, 1, rows // 2, width), lambda j, s: (0, j, 0, 0))
        out = (half, half, jax.ShapeDtypeStruct((prompts, group, rows), jnp.float32))
        out_specs = (half_spec, half_spec, pl.BlockSpec((1, group, rows), lambda j, s: (j, 0, 0)))
    else:
        out = (jax.ShapeDtypeStruct((prompts, rows * group, width), jnp.float32),) * 2
        out_specs = (state, state)
    work = prompts * most // 2 * rows * group * tokens
    return pl.pallas_call(
        functools.partial(
            attend_kernel, width**-0.5, len(keys), before is None, before is not None, values_at
        ),
        out_shape=out,
        grid_spec=pltpu.PrefetchScalarGridSpec(
            num_scalar_prefetch=1,
            grid=(prompts,),
            in_specs=[pl.BlockSpec((1, rows, features), lambda j, s: (j, 0, 0)), table, table]
            + [whole] * (len(keys) + len(values))
            + ([state, state] if before else []),
            out_specs=out_specs,
            scratch_shapes=[
                pltpu.VMEM((rows * group, width), jnp.bfloat16),
                pltpu.VMEM((tokens, width), jnp.bfloat16),
                pltpu.VMEM((2 * tokens, width), jnp.bfloat16),
                pltpu.VMEM((2 * tokens, 2 * width), jnp.bfloat16),
                pltpu.VMEM((most // 2, rows * group, 2 * tokens), jnp.float32),
                pltpu.VMEM((rows * group, width), jnp.float32),
                pltpu.VMEM((rows * group, 2 * width), jnp.float32),
                pltpu.SMEM((most + 1,), jnp.int32),
                pltpu.SMEM((most + 1,), jnp.int32),
            ],
        ),
        cost_estimate=pl.CostEstimate(
            flops=4 * work * width, bytes_accessed=8 * work, transcendentals=work
        ),
        compiler_params=pltpu.CompilerParams(vmem_limit_bytes=48 * 1024 * 1024),
    )(slots, query, cosine, sine, *keys, *values, *(before or ()))


def project_kernel(rows_ref, weight_ref, out_ref):
    columns, heads = rows_ref.shape[:2]
    left = jnp.concatenate(
        [
            jnp.concatenate([rows_ref[d, h] for h in range(heads)], axis=1)
            for d in range(columns)
        ],
        axis=0,
    )
    right = jnp.concatenate([weight_ref[h, 0] for h in range(heads)], axis=0)
    out_ref[0] = jnp.dot(left, right, preferred_element_type=jnp.float32).astype(out_ref.dtype)


def project(rows_in, weight):
    columns, heads, rows, width = rows_in.shape
    owners, out_columns = weight.shape[1], weight.shape[3]
    return pl.pallas_call(
        project_kernel,
        out_shape=jax.ShapeDtypeStruct((owners, columns * rows, out_columns), jnp.bfloat16),
        grid=(owners,),
        in_specs=[
            pl.BlockSpec((columns, heads, rows, width), lambda s: (0, 0, 0, 0)),
            pl.BlockSpec((heads, 1, width, out_columns), lambda s: (0, s, 0, 0)),
        ],
        out_specs=pl.BlockSpec((1, columns * rows, out_columns), lambda s: (s, 0, 0)),
        compiler_params=pltpu.CompilerParams(vmem_limit_bytes=60 * 1024 * 1024),
    )(rows_in, weight)


def merged(outs, lses):
    top = jnp.max(lses, axis=0)
    share = jnp.exp(lses - top)
    total = jnp.sum(share, axis=0)
    share = share / total
    out = jnp.sum(outs.astype(jnp.float32) * share[..., None], axis=0)
    return out, top + jnp.log(total)


def three_parts(value):
    first = lax.reduce_precision(value, 8, 7)
    rest = value - first
    second = lax.reduce_precision(rest, 8, 7)
    return jnp.stack([first, second, rest - second]).astype(jnp.bfloat16)


def turns(delta, width):
    half = width // 2
    inverse = theta_base ** (-2.0 * jnp.arange(half, dtype=jnp.float32) / width)
    angle = delta.astype(jnp.float32)[..., None] * inverse
    cosine, sine = jnp.cos(angle), jnp.sin(angle)
    return jnp.concatenate([cosine, cosine], axis=-1), jnp.concatenate([-sine, sine], axis=-1)


def body(
    queries, passage_keys, passage_values, offsets, out_weight, passage_list, targets, row_counts
):
    rows_of, columns = lax.axis_size(ROW), lax.axis_size(COL)
    y, x, c = lax.axis_index(ROW), lax.axis_index(COL), lax.axis_index("ctx")
    z = lax.axis_index("head")
    held, tokens, width = passage_keys.shape
    listed = passage_list.shape[1]
    prompt_rows, features = queries.shape[1:]
    group = features // width
    halves = lax.axis_size("ctx")
    half_rows = prompt_rows // halves

    tail = jnp.pad(jnp.stack(coded(offsets)), ((0, 14), (0, width - held)))
    own = jnp.concatenate(
        [passage_keys.reshape(-1, width), tail, passage_values.reshape(-1, width)], axis=0
    )
    values_at = held * tokens + 16
    pieces = {0: own, 1: shift(own, COL, -1), 3: shift(own, COL, 1)}
    opposite = (
        shift(pieces[3][:values_at], COL, 1),
        shift(pieces[1][values_at:], COL, -1),
    )

    asked = jnp.concatenate([passage_list[0], targets[0], row_counts])
    asked = jnp.stack(coded(asked))
    asked = jnp.pad(asked, ((0, 14), (0, features - asked.shape[1])))
    query = jnp.concatenate([queries, asked[None]], axis=1)
    query = lax.all_gather(query, ROW, axis=0, tiled=True)
    query, pieces = lax.optimization_barrier((query, pieces))
    asked = decoded(query[:, prompt_rows], query[:, prompt_rows + 1])
    weight = out_weight.reshape(group, width, -1)
    weight = lax.all_to_all(weight, ROW, split_axis=0, concat_axis=0, tiled=True)
    weight = lax.all_gather(weight[None], "head", axis=0, tiled=True)

    local = asked[:, :listed] - y * columns * held
    mine = (local >= 0) & (local < columns * held)
    ahead = (local // held - x) % columns
    within = local % held

    def tables(order, pieces):
        slots = jnp.full_like(within, -1)
        for at, d in enumerate(order):
            slots = jnp.where(mine & (ahead == d), at * held + within, slots)
        tails = jnp.stack([p[held * tokens : held * tokens + 2, :held] for p in pieces])
        near = decoded(tails[:, 0], tails[:, 1]).reshape(-1)
        same = slots[..., None] == jnp.arange(len(order) * held, dtype=jnp.int32)
        moved = asked[:, listed : 2 * listed] - jnp.sum(jnp.where(same, near, 0), axis=-1)
        return (slots.reshape(-1), *turns(moved, width))

    early = (0, 1, 3)
    pieces = [pieces[d] for d in early]
    slots, cosine, sine = tables(early, pieces)
    sizes = (prompt_rows, tokens, values_at)
    before = attend(slots, query, cosine, sine, pieces, [], None, *sizes)
    before, opposite = lax.optimization_barrier((before, opposite))
    slots, cosine, sine = tables((2,), opposite[:1])
    slots = jnp.concatenate([slots, c[None]])
    out, other, lse = attend(
        slots, query, cosine, sine, opposite[:1], opposite[1:], before, *sizes
    )

    lse = jnp.transpose(lse.reshape(rows_of, group, halves, half_rows), (2, 1, 0, 3))
    swap = [(i, 1 - i) for i in range(2)]
    pick = functools.partial(lax.dynamic_index_in_dim, axis=0, keepdims=False)
    other = lax.ppermute(other, "ctx", swap)
    other_lse = lax.ppermute(pick(lse, 1 - c), "ctx", swap)
    out, lse = merged(jnp.stack([out, other]), jnp.stack([pick(lse, c), other_lse]))

    out = out.astype(jnp.bfloat16).reshape(group * rows_of, half_rows, width)
    parts = jnp.moveaxis(three_parts(lse.reshape(group * rows_of, half_rows)), 0, 1)
    parts = jnp.pad(parts, ((0, 0), (0, 5), (0, width - half_rows)))
    sent = jnp.concatenate([out, parts], axis=1)
    count = lax.dynamic_index_in_dim(asked[:, 2 * listed], z, keepdims=False)
    live = c * half_rows + jnp.arange(half_rows, dtype=jnp.int32) < count
    sent, live = lax.optimization_barrier((sent, live))
    got = lax.all_to_all(sent, (ROW, "head"), split_axis=0, concat_axis=0, tiled=True)
    got = got.reshape(rows_of, -1, half_rows + 8, width)
    lses = got[:, :, half_rows : half_rows + 3, :half_rows].astype(jnp.float32)
    attended, _ = merged(got[:, :, :half_rows], jnp.sum(lses, axis=2))
    attended = jnp.where(live[:, None], attended, 0.0).astype(jnp.bfloat16)

    rows_in = lax.all_gather(attended[None], COL, axis=0, tiled=True)
    terms = project(rows_in, weight)
    terms = lax.all_to_all(terms, ROW, split_axis=0, concat_axis=0, tiled=True)
    total = jnp.sum(terms.astype(jnp.float32), axis=0)
    return total.astype(jnp.bfloat16)[None]


def solution(mesh):
    finer = Mesh(
        mesh.devices.reshape(8, 4, mesh.shape["ctx"], mesh.shape["head"]),
        ("lib_0", "lib_1", "ctx", "head"),
    )
    return jax.shard_map(
        body,
        mesh=finer,
        in_specs=(
            P(LIB, None, "head"),
            P(LIB, "ctx", "head"),
            P(LIB, "ctx", "head"),
            P(LIB),
            P("head", LIB),
            P(LIB, None),
            P(LIB, None),
            P(LIB),
        ),
        out_specs=P("ctx", "head", LIB),
        check_vma=False,
    )
```

```python
import functools

import jax
import jax.numpy as jnp
from jax import lax
from jax.experimental import pallas as pl
from jax.experimental.pallas import tpu as pltpu
from jax.sharding import Mesh
from jax.sharding import PartitionSpec as P

ROW, COL = "lib_0", "lib_1"
LIB = (ROW, COL)
theta_base = 500000.0
EMPTY = -1e30
CHUNK = 256
MOST = 2


def shift(value, axis, by):
    n = lax.axis_size(axis)
    return lax.ppermute(value, axis, [(i, (i + by) % n) for i in range(n)])


def coded(integers):
    return (integers // 128).astype(jnp.bfloat16), (integers % 128).astype(jnp.bfloat16)


def decoded(high, low):
    return high.astype(jnp.int32) * 128 + low.astype(jnp.int32)


def attend_kernel(scale, pieces, first, last, slot_ref, q_ref, cos_ref, sin_ref, *refs):
    key_refs, value_refs, refs = refs[:pieces], refs[pieces : 2 * pieces], refs[2 * pieces :]
    if not first:
        (before_ref, before_lse_ref), refs = refs[:2], refs[2:]
    out_ref, lse_ref, q_scr, tile, k_scr, v_scr, s_scr, m_scr, acc_scr, used, entry = refs
    prompt = pl.program_id(0)
    listed, width = cos_ref.shape[1:]
    rows = q_ref.shape[1]
    group = q_ref.shape[2] // width
    total_rows = rows * group
    tokens = tile.shape[0]
    held = key_refs[0].shape[0] // tokens
    factor = scale * 1.4426950408889634
    chunks = [slice(r, r + CHUNK) for r in range(0, total_rows, CHUNK)]

    @pl.when(prompt == 0)
    def _():
        v_scr[:, width:] = jnp.ones((2 * tokens, width), v_scr.dtype)

    for g in range(group):
        q_scr[g * rows : (g + 1) * rows] = q_ref[0, :, g * width : (g + 1) * width]
    for span in chunks:
        if first:
            m_scr[span] = jnp.full((CHUNK, width), EMPTY, jnp.float32)
        else:
            m_scr[span] = before_lse_ref[0, span] * (1.0 / scale)

    def note(k, count):
        slot = slot_ref[prompt * listed + k]
        used[count] = slot
        entry[count] = k
        return count + jnp.where(slot >= 0, 1, 0)

    count = lax.fori_loop(0, listed, note, 0)
    pairs = (count + 1) // 2

    def fetch(refs, slot):
        def at(index):
            return pl.ds(pl.multiple_of(index * tokens, tokens), tokens)

        if pieces == 1:
            return refs[0][at(slot)]
        for d in range(pieces):

            @pl.when(slot // held == d)
            def _():
                tile[...] = refs[d][at(slot % held)]

        return tile[...]

    def score(t, carry):
        for b in range(2):
            i = jnp.minimum(2 * t + b, count - 1)
            keys = fetch(key_refs, used[i]).astype(jnp.float32)
            cosine = cos_ref[0, pl.ds(entry[i], 1), :]
            sine = sin_ref[0, pl.ds(entry[i], 1), :]
            turned = keys * cosine + pltpu.roll(keys, width // 2, 1) * sine
            k_scr[b * tokens : (b + 1) * tokens] = turned.astype(jnp.bfloat16)
        both = 2 * t + 1 < count
        for span in chunks:
            s = lax.dot_general(
                q_scr[span],
                k_scr[...],
                (((1,), (1,)), ((), ())),
                preferred_element_type=jnp.float32,
            )
            highest = m_scr[span]
            for u in range(0, 2 * tokens, width):
                part = s[:, u : u + width]
                if u >= tokens:
                    part = jnp.where(both, part, EMPTY)
                s_scr[t, span, u : u + width] = part
                highest = jnp.maximum(highest, part)
            m_scr[span] = highest
        return carry

    lax.fori_loop(0, pairs, score, 0)
    for span in chunks:
        m = jnp.broadcast_to(jnp.max(m_scr[span], axis=1, keepdims=True), (CHUNK, width))
        m_scr[span] = m
        if first:
            acc_scr[span] = jnp.zeros((CHUNK, 2 * width), jnp.float32)
        else:
            weight = jnp.exp2((before_lse_ref[0, span] * (1.0 / scale) - m) * factor)
            acc_scr[span, :width] = before_ref[0, span] * weight
            acc_scr[span, width:] = weight

    def weigh(t, carry):
        for b in range(2):
            i = jnp.minimum(2 * t + b, count - 1)
            v_scr[b * tokens : (b + 1) * tokens, :width] = fetch(value_refs, used[i])
        for span in chunks:
            m = m_scr[span]
            parts = [
                jnp.exp2((s_scr[t, span, u : u + width] - m) * factor)
                for u in range(0, 2 * tokens, width)
            ]
            weights = jnp.concatenate([p.astype(jnp.bfloat16) for p in parts], axis=1)
            acc_scr[span] += jnp.dot(weights, v_scr[...], preferred_element_type=jnp.float32)
        return carry

    lax.fori_loop(0, pairs, weigh, 0)
    row = lax.broadcasted_iota(jnp.int32, (rows, rows), 0)
    column = lax.broadcasted_iota(jnp.int32, (rows, rows), 1)
    for g in range(group):
        span = slice(g * rows, (g + 1) * rows)
        total = acc_scr[span, width:]
        if first:
            total = jnp.where(count == 0, 1.0, total)
        out = acc_scr[span, :width] / total
        lse = m_scr[span] * scale + jnp.log(total)
        if last:
            halves = out_ref.shape[0]
            part = rows // halves
            for c in range(halves):
                out_ref[c, g, 0] = out[c * part : (c + 1) * part].astype(out_ref.dtype)
            lse_ref[0, g : g + 1, :] = jnp.sum(
                jnp.where(row == column, lse, 0.0), axis=0, keepdims=True
            )
        else:
            out_ref[0, span] = out
            lse_ref[0, span] = lse


def attend(slots, query, cosine, sine, keys, values, before, halves, rows, tokens):
    prompts, _, features = query.shape
    listed, width = cosine.shape[1:]
    group = features // width
    most = MOST * len(keys)
    whole = pl.BlockSpec(memory_space=pltpu.VMEM)
    table = pl.BlockSpec((1, listed, width), lambda j, s: (j, 0, 0))
    state = pl.BlockSpec((1, rows * group, width), lambda j, s: (j, 0, 0))
    if halves:
        part = rows // halves
        out = (
            jax.ShapeDtypeStruct((halves, group, prompts, part, width), jnp.bfloat16),
            jax.ShapeDtypeStruct((prompts, group, rows), jnp.float32),
        )
        out_specs = (
            pl.BlockSpec((halves, group, 1, part, width), lambda j, s: (0, 0, j, 0, 0)),
            pl.BlockSpec((1, group, rows), lambda j, s: (j, 0, 0)),
        )
    else:
        out = (jax.ShapeDtypeStruct((prompts, rows * group, width), jnp.float32),) * 2
        out_specs = (state, state)
    work = prompts * most // 2 * rows * group * tokens
    return pl.pallas_call(
        functools.partial(attend_kernel, width**-0.5, len(keys), before is None, bool(halves)),
        out_shape=out,
        grid_spec=pltpu.PrefetchScalarGridSpec(
            num_scalar_prefetch=1,
            grid=(prompts,),
            in_specs=[pl.BlockSpec((1, rows, features), lambda j, s: (j, 0, 0)), table, table]
            + [whole] * (2 * len(keys))
            + ([state, state] if before else []),
            out_specs=out_specs,
            scratch_shapes=[
                pltpu.VMEM((rows * group, width), jnp.bfloat16),
                pltpu.VMEM((tokens, width), jnp.bfloat16),
                pltpu.VMEM((2 * tokens, width), jnp.bfloat16),
                pltpu.VMEM((2 * tokens, 2 * width), jnp.bfloat16),
                pltpu.VMEM((most // 2, rows * group, 2 * tokens), jnp.float32),
                pltpu.VMEM((rows * group, width), jnp.float32),
                pltpu.VMEM((rows * group, 2 * width), jnp.float32),
                pltpu.SMEM((most + 1,), jnp.int32),
                pltpu.SMEM((most + 1,), jnp.int32),
            ],
        ),
        cost_estimate=pl.CostEstimate(
            flops=4 * work * width, bytes_accessed=8 * work, transcendentals=work
        ),
        compiler_params=pltpu.CompilerParams(vmem_limit_bytes=48 * 1024 * 1024),
    )(slots, query, cosine, sine, *keys, *values, *(before or ()))


def project_kernel(rows_ref, weight_ref, out_ref):
    columns, heads = rows_ref.shape[:2]
    left = jnp.concatenate(
        [
            jnp.concatenate([rows_ref[d, h] for h in range(heads)], axis=1)
            for d in range(columns)
        ],
        axis=0,
    )
    right = jnp.concatenate([weight_ref[h, 0] for h in range(heads)], axis=0)
    out_ref[0] = jnp.dot(left, right, preferred_element_type=jnp.float32).astype(out_ref.dtype)


def project(rows_in, weight):
    columns, heads, rows, width = rows_in.shape
    owners, out_columns = weight.shape[1], weight.shape[3]
    return pl.pallas_call(
        project_kernel,
        out_shape=jax.ShapeDtypeStruct((owners, columns * rows, out_columns), jnp.bfloat16),
        grid=(owners,),
        in_specs=[
            pl.BlockSpec((columns, heads, rows, width), lambda s: (0, 0, 0, 0)),
            pl.BlockSpec((heads, 1, width, out_columns), lambda s: (0, s, 0, 0)),
        ],
        out_specs=pl.BlockSpec((1, columns * rows, out_columns), lambda s: (s, 0, 0)),
        compiler_params=pltpu.CompilerParams(vmem_limit_bytes=32 * 1024 * 1024),
    )(rows_in, weight)


def merged(outs, lses):
    top = jnp.max(lses, axis=0)
    share = jnp.exp(lses - top)
    total = jnp.sum(share, axis=0)
    share = share / total
    out = jnp.sum(outs.astype(jnp.float32) * share[..., None], axis=0)
    return out, top + jnp.log(total)


def three_parts(value):
    first = lax.reduce_precision(value, 8, 7)
    rest = value - first
    second = lax.reduce_precision(rest, 8, 7)
    return jnp.stack([first, second, rest - second]).astype(jnp.bfloat16)


def turns(delta, width):
    half = width // 2
    inverse = theta_base ** (-2.0 * jnp.arange(half, dtype=jnp.float32) / width)
    angle = delta.astype(jnp.float32)[..., None] * inverse
    cosine, sine = jnp.cos(angle), jnp.sin(angle)
    return jnp.concatenate([cosine, cosine], axis=-1), jnp.concatenate([-sine, sine], axis=-1)


def body(
    queries, passage_keys, passage_values, offsets, out_weight, passage_list, targets, row_counts
):
    rows_of, columns = lax.axis_size(ROW), lax.axis_size(COL)
    y, x, c = lax.axis_index(ROW), lax.axis_index(COL), lax.axis_index("ctx")
    z = lax.axis_index("head")
    held, tokens, width = passage_keys.shape
    listed = passage_list.shape[1]
    prompt_rows, features = queries.shape[1:]
    group = features // width
    halves = lax.axis_size("ctx")
    half_rows = prompt_rows // halves

    behind = jnp.pad(jnp.stack(coded(offsets)), ((0, 14), (0, width - held)))
    own_keys = jnp.concatenate([passage_keys.reshape(-1, width), behind], axis=0)
    own_values = passage_values.reshape(-1, width)
    keys = [own_keys, shift(own_keys, COL, -1), None, shift(own_keys, COL, 1)]
    values = [own_values, shift(own_values, COL, -1), None, shift(own_values, COL, 1)]
    keys[2] = shift(keys[3], COL, 1)
    values[2] = shift(values[1], COL, -1)

    asked = jnp.concatenate([passage_list[0], targets[0], row_counts])
    asked = jnp.stack(coded(asked))
    padded = jnp.pad(asked, ((0, 14), (0, features - asked.shape[1])))
    query = jnp.concatenate([queries, padded[None]], axis=1)
    query = lax.all_gather(query, ROW, axis=0, tiled=True)
    asked = query[:, prompt_rows : prompt_rows + 2, : asked.shape[1]]
    asked, keys[1], near_keys = lax.optimization_barrier((asked, keys[1], keys[3]))
    asked = decoded(asked[:, 0], asked[:, 1])
    weight, _ = lax.optimization_barrier((out_weight, keys[3]))
    weight = weight.reshape(group, width, -1)
    weight = lax.all_to_all(weight, ROW, split_axis=0, concat_axis=0, tiled=True)
    weight = lax.all_gather(weight[None], "head", axis=0, tiled=True)

    keys[3] = near_keys
    local = asked[:, :listed] - y * columns * held
    mine = (local >= 0) & (local < columns * held)
    ahead = (local // held - x) % columns
    within = local % held

    def tables(order, pieces):
        slots = jnp.full_like(within, -1)
        for at, d in enumerate(order):
            slots = jnp.where(mine & (ahead == d), at * held + within, slots)
        tails = jnp.stack([p[held * tokens : held * tokens + 2, :held] for p in pieces])
        near = decoded(tails[:, 0], tails[:, 1]).reshape(-1)
        same = slots[..., None] == jnp.arange(len(order) * held, dtype=jnp.int32)
        moved = asked[:, listed : 2 * listed] - jnp.sum(jnp.where(same, near, 0), axis=-1)
        return (slots.reshape(-1), *turns(moved, width))

    before = None
    for order, laid_out in (((0, 1, 3), 0), ((2,), halves)):
        pieces = [keys[d] for d in order]
        if before is not None:
            before, pieces = lax.optimization_barrier((before, pieces))
        slots, cosine, sine = tables(order, pieces)
        before = attend(
            slots, query, cosine, sine, pieces, [values[d] for d in order], before, laid_out,
            prompt_rows, tokens,
        )
    out, lse = before

    lse = jnp.transpose(lse.reshape(rows_of, group, halves, half_rows), (2, 1, 0, 3))
    swap = [(i, 1 - i) for i in range(2)]
    pick = functools.partial(lax.dynamic_index_in_dim, axis=0, keepdims=False)
    other = lax.ppermute(pick(out, 1 - c), "ctx", swap)
    other_lse = lax.ppermute(pick(lse, 1 - c), "ctx", swap)
    out, lse = merged(
        jnp.stack([pick(out, c), other]), jnp.stack([pick(lse, c), other_lse])
    )

    out = out.astype(jnp.bfloat16).reshape(group * rows_of, half_rows, width)
    parts = jnp.moveaxis(three_parts(lse.reshape(group * rows_of, half_rows)), 0, 1)
    parts = jnp.pad(parts, ((0, 0), (0, 5), (0, width - half_rows)))
    sent = jnp.concatenate([out, parts], axis=1)
    count = lax.dynamic_index_in_dim(asked[:, 2 * listed], z, keepdims=False)
    live = c * half_rows + jnp.arange(half_rows, dtype=jnp.int32) < count
    sent, live = lax.optimization_barrier((sent, live))
    got = lax.all_to_all(sent, (ROW, "head"), split_axis=0, concat_axis=0, tiled=True)
    got, weight = lax.optimization_barrier((got, weight))
    got = got.reshape(rows_of, -1, half_rows + 8, width)
    lses = got[:, :, half_rows : half_rows + 3, :half_rows].astype(jnp.float32)
    attended, _ = merged(got[:, :, :half_rows], jnp.sum(lses, axis=2))
    attended = jnp.where(live[:, None], attended, 0.0).astype(jnp.bfloat16)

    rows_in = lax.all_gather(attended[None], COL, axis=0, tiled=True)
    terms = project(rows_in, weight)
    terms = lax.all_to_all(terms, ROW, split_axis=0, concat_axis=0, tiled=True)
    total = jnp.sum(terms.astype(jnp.float32), axis=0)
    return total.astype(jnp.bfloat16)[None]


def solution(mesh):
    finer = Mesh(
        mesh.devices.reshape(8, 4, mesh.shape["ctx"], mesh.shape["head"]),
        ("lib_0", "lib_1", "ctx", "head"),
    )
    return jax.shard_map(
        body,
        mesh=finer,
        in_specs=(
            P(LIB, None, "head"),
            P(LIB, "ctx", "head"),
            P(LIB, "ctx", "head"),
            P(LIB),
            P("head", LIB),
            P(LIB, None),
            P(LIB, None),
            P(LIB),
        ),
        out_specs=P("ctx", "head", LIB),
        check_vma=False,
    )
```

```python
import functools

import jax
import jax.numpy as jnp
from jax import lax
from jax.experimental import pallas as pl
from jax.experimental.pallas import tpu as pltpu
from jax.sharding import Mesh
from jax.sharding import PartitionSpec as P

ROW, COL = "lib_0", "lib_1"
LIB = (ROW, COL)
theta_base = 500000.0
EMPTY = -1e30
CHUNK = 256
MOST = 2


def shift(value, axis, by):
    n = lax.axis_size(axis)
    return lax.ppermute(value, axis, [(i, (i + by) % n) for i in range(n)])


def coded(integers):
    return (integers // 128).astype(jnp.bfloat16), (integers % 128).astype(jnp.bfloat16)


def decoded(high, low):
    return high.astype(jnp.int32) * 128 + low.astype(jnp.int32)


def attend_kernel(scale, pieces, first, last, slot_ref, q_ref, cos_ref, sin_ref, *refs):
    key_refs, value_refs, refs = refs[:pieces], refs[pieces : 2 * pieces], refs[2 * pieces :]
    if not first:
        (before_ref, before_top_ref), refs = refs[:2], refs[2:]
    out_ref, lse_ref, q_scr, tile, k_scr, v_scr, s_scr, m_scr, acc_scr, used, entry = refs
    if not last:
        acc_scr, m_scr = out_ref.at[0], lse_ref.at[0]
    prompt = pl.program_id(0)
    listed, width = cos_ref.shape[1:]
    rows = q_ref.shape[1]
    group = q_ref.shape[2] // width
    total_rows = rows * group
    tokens = tile.shape[0]
    held = key_refs[0].shape[0] // tokens
    factor = scale * 1.4426950408889634
    chunks = [slice(r, r + CHUNK) for r in range(0, total_rows, CHUNK)]

    @pl.when(prompt == 0)
    def _():
        v_scr[:, width:] = jnp.ones((2 * tokens, width), v_scr.dtype)

    for g in range(group):
        q_scr[g * rows : (g + 1) * rows] = q_ref[0, :, g * width : (g + 1) * width]
    for span in chunks:
        if first:
            m_scr[span] = jnp.full((CHUNK, width), EMPTY, jnp.float32)
        else:
            m_scr[span] = before_top_ref[0, span]

    def note(k, count):
        slot = slot_ref[prompt * listed + k]
        used[count] = slot
        entry[count] = k
        return count + jnp.where(slot >= 0, 1, 0)

    count = lax.fori_loop(0, listed, note, 0)
    pairs = (count + 1) // 2

    def fetch(refs, slot):
        def at(index):
            return pl.ds(pl.multiple_of(index * tokens, tokens), tokens)

        if pieces == 1:
            return refs[0][at(slot)]
        for d in range(pieces):

            @pl.when(slot // held == d)
            def _():
                tile[...] = refs[d][at(slot % held)]

        return tile[...]

    def score(t, carry):
        for b in range(2):
            i = jnp.minimum(2 * t + b, count - 1)
            keys = fetch(key_refs, used[i]).astype(jnp.float32)
            cosine = cos_ref[0, pl.ds(entry[i], 1), :]
            sine = sin_ref[0, pl.ds(entry[i], 1), :]
            turned = keys * cosine + pltpu.roll(keys, width // 2, 1) * sine
            k_scr[b * tokens : (b + 1) * tokens] = turned.astype(jnp.bfloat16)
        both = 2 * t + 1 < count
        for span in chunks:
            s = lax.dot_general(
                q_scr[span],
                k_scr[...],
                (((1,), (1,)), ((), ())),
                preferred_element_type=jnp.float32,
            )
            highest = m_scr[span]
            for u in range(0, 2 * tokens, width):
                part = s[:, u : u + width]
                if u >= tokens:
                    part = jnp.where(both, part, EMPTY)
                s_scr[t, span, u : u + width] = part
                highest = jnp.maximum(highest, part)
            m_scr[span] = highest
        return carry

    lax.fori_loop(0, pairs, score, 0)
    for span in chunks:
        m = jnp.broadcast_to(jnp.max(m_scr[span], axis=1, keepdims=True), (CHUNK, width))
        m_scr[span] = m
        if first:
            acc_scr[span] = jnp.zeros((CHUNK, 2 * width), jnp.float32)
        else:
            weight = jnp.exp2((before_top_ref[0, span] - m) * factor)
            for u in (0, width):
                acc_scr[span, u : u + width] = before_ref[0, span, u : u + width] * weight

    def weigh(t, carry):
        for b in range(2):
            i = jnp.minimum(2 * t + b, count - 1)
            v_scr[b * tokens : (b + 1) * tokens, :width] = fetch(value_refs, used[i])
        for span in chunks:
            m = m_scr[span]
            parts = [
                jnp.exp2((s_scr[t, span, u : u + width] - m) * factor)
                for u in range(0, 2 * tokens, width)
            ]
            weights = jnp.concatenate([p.astype(jnp.bfloat16) for p in parts], axis=1)
            acc_scr[span] += jnp.dot(weights, v_scr[...], preferred_element_type=jnp.float32)
        return carry

    lax.fori_loop(0, pairs, weigh, 0)
    if not last:
        return
    halves = out_ref.shape[0]
    part = rows // halves
    row = lax.broadcasted_iota(jnp.int32, (rows, rows), 0)
    column = lax.broadcasted_iota(jnp.int32, (rows, rows), 1)

    def line(value):
        return jnp.sum(jnp.where(row == column, value, 0.0), axis=0, keepdims=True)

    tops, totals = [], []
    for g in range(group):
        span = slice(g * rows, (g + 1) * rows)
        total = jnp.maximum(acc_scr[span, width:], 1.0)
        out = (acc_scr[span, :width] / total).astype(out_ref.dtype)
        for c in range(halves):
            out_ref[c, g, 0] = out[c * part : (c + 1) * part]
        tops.append(line(m_scr[span]))
        totals.append(line(total))
    tops, totals = jnp.concatenate(tops, axis=0), jnp.concatenate(totals, axis=0)
    lse_ref[0] = tops * scale + jnp.log(totals)


def attend(slots, query, cosine, sine, keys, values, before, halves, rows, tokens):
    prompts, _, features = query.shape
    listed, width = cosine.shape[1:]
    group = features // width
    most = MOST * len(keys)
    whole = pl.BlockSpec(memory_space=pltpu.VMEM)
    table = pl.BlockSpec((1, listed, width), lambda j, s: (j, 0, 0))
    state = [
        pl.BlockSpec((1, rows * group, w * width), lambda j, s: (j, 0, 0)) for w in (2, 1)
    ]
    if halves:
        part = rows // halves
        out = (
            jax.ShapeDtypeStruct((halves, group, prompts, part, width), jnp.bfloat16),
            jax.ShapeDtypeStruct((prompts, group, rows), jnp.float32),
        )
        out_specs = (
            pl.BlockSpec((halves, group, 1, part, width), lambda j, s: (0, 0, j, 0, 0)),
            pl.BlockSpec((1, group, rows), lambda j, s: (j, 0, 0)),
        )
    else:
        out = tuple(
            jax.ShapeDtypeStruct((prompts, rows * group, w * width), jnp.float32) for w in (2, 1)
        )
        out_specs = tuple(state)
    work = prompts * most // 2 * rows * group * tokens
    return pl.pallas_call(
        functools.partial(attend_kernel, width**-0.5, len(keys), before is None, bool(halves)),
        out_shape=out,
        grid_spec=pltpu.PrefetchScalarGridSpec(
            num_scalar_prefetch=1,
            grid=(prompts,),
            in_specs=[pl.BlockSpec((1, rows, features), lambda j, s: (j, 0, 0)), table, table]
            + [whole] * (2 * len(keys))
            + (state if before else []),
            out_specs=out_specs,
            scratch_shapes=[
                pltpu.VMEM((rows * group, width), jnp.bfloat16),
                pltpu.VMEM((tokens, width), jnp.bfloat16),
                pltpu.VMEM((2 * tokens, width), jnp.bfloat16),
                pltpu.VMEM((2 * tokens, 2 * width), jnp.bfloat16),
                pltpu.VMEM((most // 2, rows * group, 2 * tokens), jnp.float32),
                pltpu.VMEM((rows * group, width), jnp.float32),
                pltpu.VMEM((rows * group, 2 * width), jnp.float32),
                pltpu.SMEM((most + 1,), jnp.int32),
                pltpu.SMEM((most + 1,), jnp.int32),
            ],
        ),
        cost_estimate=pl.CostEstimate(
            flops=4 * work * width, bytes_accessed=8 * work, transcendentals=work
        ),
        compiler_params=pltpu.CompilerParams(vmem_limit_bytes=48 * 1024 * 1024),
    )(slots, query, cosine, sine, *keys, *values, *(before or ()))


def project_kernel(rows_ref, weight_ref, out_ref):
    columns, heads = rows_ref.shape[:2]
    left = jnp.concatenate(
        [
            jnp.concatenate([rows_ref[d, h] for h in range(heads)], axis=1)
            for d in range(columns)
        ],
        axis=0,
    )
    right = jnp.concatenate([weight_ref[h, 0] for h in range(heads)], axis=0)
    out_ref[0] = jnp.dot(left, right, preferred_element_type=jnp.float32).astype(out_ref.dtype)


def project(rows_in, weight):
    columns, heads, rows, width = rows_in.shape
    owners, out_columns = weight.shape[1], weight.shape[3]
    return pl.pallas_call(
        project_kernel,
        out_shape=jax.ShapeDtypeStruct((owners, columns * rows, out_columns), jnp.bfloat16),
        grid=(owners,),
        in_specs=[
            pl.BlockSpec((columns, heads, rows, width), lambda s: (0, 0, 0, 0)),
            pl.BlockSpec((heads, 1, width, out_columns), lambda s: (0, s, 0, 0)),
        ],
        out_specs=pl.BlockSpec((1, columns * rows, out_columns), lambda s: (s, 0, 0)),
        compiler_params=pltpu.CompilerParams(vmem_limit_bytes=32 * 1024 * 1024),
    )(rows_in, weight)


def merged(outs, lses):
    top = jnp.max(lses, axis=0)
    share = jnp.exp(lses - top)
    total = jnp.sum(share, axis=0)
    share = share / total
    out = jnp.sum(outs.astype(jnp.float32) * share[..., None], axis=0)
    return out, top + jnp.log(total)


def three_parts(value):
    first = lax.reduce_precision(value, 8, 7)
    rest = value - first
    second = lax.reduce_precision(rest, 8, 7)
    return jnp.stack([first, second, rest - second]).astype(jnp.bfloat16)


def turns(delta, width):
    half = width // 2
    inverse = theta_base ** (-2.0 * jnp.arange(half, dtype=jnp.float32) / width)
    angle = delta.astype(jnp.float32)[..., None] * inverse
    cosine, sine = jnp.cos(angle), jnp.sin(angle)
    return jnp.concatenate([cosine, cosine], axis=-1), jnp.concatenate([-sine, sine], axis=-1)


def body(
    queries, passage_keys, passage_values, offsets, out_weight, passage_list, targets, row_counts
):
    rows_of, columns = lax.axis_size(ROW), lax.axis_size(COL)
    y, x, c = lax.axis_index(ROW), lax.axis_index(COL), lax.axis_index("ctx")
    z = lax.axis_index("head")
    held, tokens, width = passage_keys.shape
    listed = passage_list.shape[1]
    prompt_rows, features = queries.shape[1:]
    group = features // width
    halves = lax.axis_size("ctx")
    half_rows = prompt_rows // halves

    behind = jnp.pad(jnp.stack(coded(offsets)), ((0, 14), (0, width - held)))
    own_keys = jnp.concatenate([passage_keys.reshape(-1, width), behind], axis=0)
    own_values = passage_values.reshape(-1, width)
    keys = [own_keys, shift(own_keys, COL, -1), None, shift(own_keys, COL, 1)]
    values = [own_values, shift(own_values, COL, -1), None, shift(own_values, COL, 1)]
    second = lax.optimization_barrier((keys[3], values[3]))[0]
    keys[2] = shift(second, COL, 1)
    second = lax.optimization_barrier((values[1], keys[1]))[0]
    values[2] = shift(second, COL, -1)

    asked = jnp.concatenate([passage_list[0], targets[0], row_counts])
    asked = jnp.stack(coded(asked))
    padded = jnp.pad(asked, ((0, 14), (0, features - asked.shape[1])))
    query = jnp.concatenate([queries, padded[None]], axis=1)
    query = lax.all_gather(query, ROW, axis=0, tiled=True)
    asked = query[:, prompt_rows : prompt_rows + 2, : asked.shape[1]]
    asked, keys[1], near_keys = lax.optimization_barrier((asked, keys[1], keys[3]))
    asked = decoded(asked[:, 0], asked[:, 1])
    weight, _ = lax.optimization_barrier((out_weight, keys[3]))
    weight = weight.reshape(group, width, -1)
    weight = lax.all_to_all(weight, ROW, split_axis=0, concat_axis=0, tiled=True)
    weight = lax.all_gather(weight[None], "head", axis=0, tiled=True)

    keys[3] = near_keys
    local = asked[:, :listed] - y * columns * held
    mine = (local >= 0) & (local < columns * held)
    ahead = (local // held - x) % columns
    within = local % held

    def tables(order, pieces):
        slots = jnp.full_like(within, -1)
        for at, d in enumerate(order):
            slots = jnp.where(mine & (ahead == d), at * held + within, slots)
        tails = jnp.stack([p[held * tokens : held * tokens + 2, :held] for p in pieces])
        near = decoded(tails[:, 0], tails[:, 1]).reshape(-1)
        same = slots[..., None] == jnp.arange(len(order) * held, dtype=jnp.int32)
        moved = asked[:, listed : 2 * listed] - jnp.sum(jnp.where(same, near, 0), axis=-1)
        return (slots.reshape(-1), *turns(moved, width))

    before = None
    for order, laid_out in (((0, 1, 3), 0), ((2,), halves)):
        pieces = [keys[d] for d in order]
        if before is not None:
            before, pieces = lax.optimization_barrier((before, pieces))
        slots, cosine, sine = tables(order, pieces)
        before = attend(
            slots, query, cosine, sine, pieces, [values[d] for d in order], before, laid_out,
            prompt_rows, tokens,
        )
    out, lse = before

    lse = jnp.transpose(lse.reshape(rows_of, group, halves, half_rows), (2, 1, 0, 3))
    swap = [(i, 1 - i) for i in range(2)]
    pick = functools.partial(lax.dynamic_index_in_dim, axis=0, keepdims=False)
    other = lax.ppermute(pick(out, 1 - c), "ctx", swap)
    other_lse = lax.ppermute(pick(lse, 1 - c), "ctx", swap)
    out, lse = merged(
        jnp.stack([pick(out, c), other]), jnp.stack([pick(lse, c), other_lse])
    )

    out = out.astype(jnp.bfloat16).reshape(group * rows_of, half_rows, width)
    parts = jnp.moveaxis(three_parts(lse.reshape(group * rows_of, half_rows)), 0, 1)
    parts = jnp.pad(parts, ((0, 0), (0, 5), (0, width - half_rows)))
    sent = jnp.concatenate([out, parts], axis=1)
    count = lax.dynamic_index_in_dim(asked[:, 2 * listed], z, keepdims=False)
    live = c * half_rows + jnp.arange(half_rows, dtype=jnp.int32) < count
    sent, live = lax.optimization_barrier((sent, live))
    got = lax.all_to_all(sent, (ROW, "head"), split_axis=0, concat_axis=0, tiled=True)
    got, weight = lax.optimization_barrier((got, weight))
    got = got.reshape(rows_of, -1, half_rows + 8, width)
    lses = got[:, :, half_rows : half_rows + 3, :half_rows].astype(jnp.float32)
    attended, _ = merged(got[:, :, :half_rows], jnp.sum(lses, axis=2))
    attended = jnp.where(live[:, None], attended, 0.0).astype(jnp.bfloat16)

    rows_in = lax.all_gather(attended[None], COL, axis=0, tiled=True)
    terms = project(rows_in, weight)
    terms = lax.all_to_all(terms, ROW, split_axis=0, concat_axis=0, tiled=True)
    total = jnp.sum(terms.astype(jnp.float32), axis=0)
    return total.astype(jnp.bfloat16)[None]


def solution(mesh):
    finer = Mesh(
        mesh.devices.reshape(8, 4, mesh.shape["ctx"], mesh.shape["head"]),
        ("lib_0", "lib_1", "ctx", "head"),
    )
    return jax.shard_map(
        body,
        mesh=finer,
        in_specs=(
            P(LIB, None, "head"),
            P(LIB, "ctx", "head"),
            P(LIB, "ctx", "head"),
            P(LIB),
            P("head", LIB),
            P(LIB, None),
            P(LIB, None),
            P(LIB),
        ),
        out_specs=P("ctx", "head", LIB),
        check_vma=False,
    )
```

```python
import functools

import jax
import jax.numpy as jnp
from jax import lax
from jax.experimental import pallas as pl
from jax.experimental.pallas import tpu as pltpu
from jax.sharding import Mesh
from jax.sharding import PartitionSpec as P

ROW, COL = "lib_0", "lib_1"
LIB = (ROW, COL)
theta_base = 500000.0
EMPTY = -1e30
CHUNK = 256
MOST = 2


def shift(value, axis, by):
    n = lax.axis_size(axis)
    return lax.ppermute(value, axis, [(i, (i + by) % n) for i in range(n)])


def coded(integers):
    return (integers // 128).astype(jnp.bfloat16), (integers % 128).astype(jnp.bfloat16)


def decoded(high, low):
    return high.astype(jnp.int32) * 128 + low.astype(jnp.int32)


def attend_kernel(scale, pieces, first, last, slot_ref, q_ref, cos_ref, sin_ref, *refs):
    key_refs, value_refs, refs = refs[:pieces], refs[pieces : 2 * pieces], refs[2 * pieces :]
    if not first:
        (before_ref, before_top_ref), refs = refs[:2], refs[2:]
    out_ref, lse_ref, q_scr, tile, k_scr, v_scr, s_scr, m_scr, acc_scr, used, entry = refs
    if not last:
        acc_scr, m_scr = out_ref.at[0], lse_ref.at[0]
    prompt = pl.program_id(0)
    listed, width = cos_ref.shape[1:]
    rows = q_ref.shape[1]
    group = q_ref.shape[2] // width
    total_rows = rows * group
    tokens = tile.shape[0]
    held = key_refs[0].shape[0] // tokens
    factor = scale * 1.4426950408889634
    chunks = [slice(r, r + CHUNK) for r in range(0, total_rows, CHUNK)]

    @pl.when(prompt == 0)
    def _():
        v_scr[:, width:] = jnp.ones((2 * tokens, width), v_scr.dtype)

    for g in range(group):
        q_scr[g * rows : (g + 1) * rows] = q_ref[0, :, g * width : (g + 1) * width]
    for span in chunks:
        if first:
            m_scr[span] = jnp.full((CHUNK, width), EMPTY, jnp.float32)
        else:
            m_scr[span] = before_top_ref[0, span]

    def note(k, count):
        slot = slot_ref[prompt * listed + k]
        used[count] = slot
        entry[count] = k
        return count + jnp.where(slot >= 0, 1, 0)

    count = lax.fori_loop(0, listed, note, 0)
    pairs = (count + 1) // 2

    def fetch(refs, slot):
        def at(index):
            return pl.ds(pl.multiple_of(index * tokens, tokens), tokens)

        if pieces == 1:
            return refs[0][at(slot)]
        for d in range(pieces):

            @pl.when(slot // held == d)
            def _():
                tile[...] = refs[d][at(slot % held)]

        return tile[...]

    def score(t, carry):
        for b in range(2):
            i = jnp.minimum(2 * t + b, count - 1)
            keys = fetch(key_refs, used[i]).astype(jnp.float32)
            cosine = cos_ref[0, pl.ds(entry[i], 1), :]
            sine = sin_ref[0, pl.ds(entry[i], 1), :]
            turned = keys * cosine + pltpu.roll(keys, width // 2, 1) * sine
            k_scr[b * tokens : (b + 1) * tokens] = turned.astype(jnp.bfloat16)
        both = 2 * t + 1 < count
        for span in chunks:
            s = lax.dot_general(
                q_scr[span],
                k_scr[...],
                (((1,), (1,)), ((), ())),
                preferred_element_type=jnp.float32,
            )
            highest = m_scr[span]
            for u in range(0, 2 * tokens, width):
                part = s[:, u : u + width]
                if u >= tokens:
                    part = jnp.where(both, part, EMPTY)
                s_scr[t, span, u : u + width] = part
                highest = jnp.maximum(highest, part)
            m_scr[span] = highest
        return carry

    lax.fori_loop(0, pairs, score, 0)
    for span in chunks:
        m = jnp.broadcast_to(jnp.max(m_scr[span], axis=1, keepdims=True), (CHUNK, width))
        m_scr[span] = m
        if first:
            acc_scr[span] = jnp.zeros((CHUNK, 2 * width), jnp.float32)
        else:
            weight = jnp.exp2((before_top_ref[0, span] - m) * factor)
            for u in (0, width):
                acc_scr[span, u : u + width] = before_ref[0, span, u : u + width] * weight

    def weigh(t, carry):
        for b in range(2):
            i = jnp.minimum(2 * t + b, count - 1)
            v_scr[b * tokens : (b + 1) * tokens, :width] = fetch(value_refs, used[i])
        for span in chunks:
            m = m_scr[span]
            parts = [
                jnp.exp2((s_scr[t, span, u : u + width] - m) * factor)
                for u in range(0, 2 * tokens, width)
            ]
            weights = jnp.concatenate([p.astype(jnp.bfloat16) for p in parts], axis=1)
            acc_scr[span] += jnp.dot(weights, v_scr[...], preferred_element_type=jnp.float32)
        return carry

    lax.fori_loop(0, pairs, weigh, 0)
    if not last:
        return
    halves = out_ref.shape[0]
    part = rows // halves
    row = lax.broadcasted_iota(jnp.int32, (rows, rows), 0)
    column = lax.broadcasted_iota(jnp.int32, (rows, rows), 1)

    def line(value):
        return jnp.sum(jnp.where(row == column, value, 0.0), axis=0, keepdims=True)

    tops, totals = [], []
    for g in range(group):
        span = slice(g * rows, (g + 1) * rows)
        total = jnp.maximum(acc_scr[span, width:], 1.0)
        out = (acc_scr[span, :width] / total).astype(out_ref.dtype)
        for c in range(halves):
            out_ref[c, g, 0] = out[c * part : (c + 1) * part]
        tops.append(line(m_scr[span]))
        totals.append(line(total))
    tops, totals = jnp.concatenate(tops, axis=0), jnp.concatenate(totals, axis=0)
    lse_ref[0] = tops * scale + jnp.log(totals)


def attend(slots, query, cosine, sine, keys, values, before, halves, rows, tokens):
    prompts, _, features = query.shape
    listed, width = cosine.shape[1:]
    group = features // width
    most = MOST * len(keys)
    whole = pl.BlockSpec(memory_space=pltpu.VMEM)
    table = pl.BlockSpec((1, listed, width), lambda j, s: (j, 0, 0))
    state = [
        pl.BlockSpec((1, rows * group, w * width), lambda j, s: (j, 0, 0)) for w in (2, 1)
    ]
    if halves:
        part = rows // halves
        out = (
            jax.ShapeDtypeStruct((halves, group, prompts, part, width), jnp.bfloat16),
            jax.ShapeDtypeStruct((prompts, group, rows), jnp.float32),
        )
        out_specs = (
            pl.BlockSpec((halves, group, 1, part, width), lambda j, s: (0, 0, j, 0, 0)),
            pl.BlockSpec((1, group, rows), lambda j, s: (j, 0, 0)),
        )
    else:
        out = tuple(
            jax.ShapeDtypeStruct((prompts, rows * group, w * width), jnp.float32) for w in (2, 1)
        )
        out_specs = tuple(state)
    work = prompts * most // 2 * rows * group * tokens
    return pl.pallas_call(
        functools.partial(attend_kernel, width**-0.5, len(keys), before is None, bool(halves)),
        out_shape=out,
        grid_spec=pltpu.PrefetchScalarGridSpec(
            num_scalar_prefetch=1,
            grid=(prompts,),
            in_specs=[pl.BlockSpec((1, rows, features), lambda j, s: (j, 0, 0)), table, table]
            + [whole] * (2 * len(keys))
            + (state if before else []),
            out_specs=out_specs,
            scratch_shapes=[
                pltpu.VMEM((rows * group, width), jnp.bfloat16),
                pltpu.VMEM((tokens, width), jnp.bfloat16),
                pltpu.VMEM((2 * tokens, width), jnp.bfloat16),
                pltpu.VMEM((2 * tokens, 2 * width), jnp.bfloat16),
                pltpu.VMEM((most // 2, rows * group, 2 * tokens), jnp.float32),
                pltpu.VMEM((rows * group, width), jnp.float32),
                pltpu.VMEM((rows * group, 2 * width), jnp.float32),
                pltpu.SMEM((most + 1,), jnp.int32),
                pltpu.SMEM((most + 1,), jnp.int32),
            ],
        ),
        cost_estimate=pl.CostEstimate(
            flops=4 * work * width, bytes_accessed=8 * work, transcendentals=work
        ),
        compiler_params=pltpu.CompilerParams(vmem_limit_bytes=48 * 1024 * 1024),
    )(slots, query, cosine, sine, *keys, *values, *(before or ()))


def project_kernel(rows_ref, weight_ref, out_ref):
    columns, heads = rows_ref.shape[:2]
    left = jnp.concatenate(
        [
            jnp.concatenate([rows_ref[d, h] for h in range(heads)], axis=1)
            for d in range(columns)
        ],
        axis=0,
    )
    right = jnp.concatenate([weight_ref[h, 0] for h in range(heads)], axis=0)
    out_ref[0] = jnp.dot(left, right, preferred_element_type=jnp.float32).astype(out_ref.dtype)


def project(rows_in, weight):
    columns, heads, rows, width = rows_in.shape
    owners, out_columns = weight.shape[1], weight.shape[3]
    return pl.pallas_call(
        project_kernel,
        out_shape=jax.ShapeDtypeStruct((owners, columns * rows, out_columns), jnp.bfloat16),
        grid=(owners,),
        in_specs=[
            pl.BlockSpec((columns, heads, rows, width), lambda s: (0, 0, 0, 0)),
            pl.BlockSpec((heads, 1, width, out_columns), lambda s: (0, s, 0, 0)),
        ],
        out_specs=pl.BlockSpec((1, columns * rows, out_columns), lambda s: (s, 0, 0)),
        compiler_params=pltpu.CompilerParams(vmem_limit_bytes=32 * 1024 * 1024),
    )(rows_in, weight)


def merged(outs, lses):
    top = jnp.max(lses, axis=0)
    share = jnp.exp(lses - top)
    total = jnp.sum(share, axis=0)
    share = share / total
    out = jnp.sum(outs.astype(jnp.float32) * share[..., None], axis=0)
    return out, top + jnp.log(total)


def three_parts(value):
    first = lax.reduce_precision(value, 8, 7)
    rest = value - first
    second = lax.reduce_precision(rest, 8, 7)
    return jnp.stack([first, second, rest - second]).astype(jnp.bfloat16)


def turns(delta, width):
    half = width // 2
    inverse = theta_base ** (-2.0 * jnp.arange(half, dtype=jnp.float32) / width)
    angle = delta.astype(jnp.float32)[..., None] * inverse
    cosine, sine = jnp.cos(angle), jnp.sin(angle)
    return jnp.concatenate([cosine, cosine], axis=-1), jnp.concatenate([-sine, sine], axis=-1)


def body(
    queries, passage_keys, passage_values, offsets, out_weight, passage_list, targets, row_counts
):
    rows_of, columns = lax.axis_size(ROW), lax.axis_size(COL)
    y, x, c = lax.axis_index(ROW), lax.axis_index(COL), lax.axis_index("ctx")
    z = lax.axis_index("head")
    held, tokens, width = passage_keys.shape
    listed = passage_list.shape[1]
    prompt_rows, features = queries.shape[1:]
    group = features // width
    halves = lax.axis_size("ctx")
    half_rows = prompt_rows // halves

    behind = jnp.pad(jnp.stack(coded(offsets)), ((0, 14), (0, width - held)))
    own_keys = jnp.concatenate([passage_keys.reshape(-1, width), behind], axis=0)
    own_values = passage_values.reshape(-1, width)
    keys = [own_keys, shift(own_keys, COL, -1), None, shift(own_keys, COL, 1)]
    values = [own_values, shift(own_values, COL, -1), None, shift(own_values, COL, 1)]
    second = lax.optimization_barrier((keys[3], values[3]))[0]
    keys[2] = shift(second, COL, 1)
    second = lax.optimization_barrier((values[1], keys[1]))[0]
    values[2] = shift(second, COL, -1)

    query = lax.all_gather(queries, ROW, axis=0, tiled=True)
    asked = jnp.stack(coded(jnp.concatenate([passage_list[0], targets[0], row_counts])))
    entries = asked.shape[1]
    asked = jnp.pad(asked, ((0, 14), (0, out_weight.shape[1] - entries)))
    asked = jnp.broadcast_to(asked, (rows_of, *asked.shape))
    weight = jnp.concatenate([out_weight.reshape(group, width, -1), asked], axis=1)
    weight = lax.all_to_all(weight, ROW, split_axis=0, concat_axis=0, tiled=True)
    asked = decoded(weight[:, width, :entries], weight[:, width + 1, :entries])
    weight = lax.all_gather(weight[None, :, :width], "head", axis=0, tiled=True)

    local = asked[:, :listed] - y * columns * held
    mine = (local >= 0) & (local < columns * held)
    ahead = (local // held - x) % columns
    within = local % held

    def tables(order, pieces):
        slots = jnp.full_like(within, -1)
        for at, d in enumerate(order):
            slots = jnp.where(mine & (ahead == d), at * held + within, slots)
        tails = jnp.stack([p[held * tokens : held * tokens + 2, :held] for p in pieces])
        near = decoded(tails[:, 0], tails[:, 1]).reshape(-1)
        same = slots[..., None] == jnp.arange(len(order) * held, dtype=jnp.int32)
        moved = asked[:, listed : 2 * listed] - jnp.sum(jnp.where(same, near, 0), axis=-1)
        return (slots.reshape(-1), *turns(moved, width))

    before = None
    for order, laid_out in (((0, 1, 3), 0), ((2,), halves)):
        pieces = [keys[d] for d in order]
        if before is not None:
            before, pieces = lax.optimization_barrier((before, pieces))
        slots, cosine, sine = tables(order, pieces)
        before = attend(
            slots, query, cosine, sine, pieces, [values[d] for d in order], before, laid_out,
            prompt_rows, tokens,
        )
    out, lse = before

    lse = jnp.transpose(lse.reshape(rows_of, group, halves, half_rows), (2, 1, 0, 3))
    swap = [(i, 1 - i) for i in range(2)]
    pick = functools.partial(lax.dynamic_index_in_dim, axis=0, keepdims=False)
    other = lax.ppermute(pick(out, 1 - c), "ctx", swap)
    other_lse = lax.ppermute(pick(lse, 1 - c), "ctx", swap)
    out, lse = merged(
        jnp.stack([pick(out, c), other]), jnp.stack([pick(lse, c), other_lse])
    )

    out = out.astype(jnp.bfloat16).reshape(group * rows_of, half_rows, width)
    parts = jnp.moveaxis(three_parts(lse.reshape(group * rows_of, half_rows)), 0, 1)
    parts = jnp.pad(parts, ((0, 0), (0, 5), (0, width - half_rows)))
    sent = jnp.concatenate([out, parts], axis=1)
    count = lax.dynamic_index_in_dim(asked[:, 2 * listed], z, keepdims=False)
    live = c * half_rows + jnp.arange(half_rows, dtype=jnp.int32) < count
    sent, live = lax.optimization_barrier((sent, live))
    got = lax.all_to_all(sent, (ROW, "head"), split_axis=0, concat_axis=0, tiled=True)
    got, weight = lax.optimization_barrier((got, weight))
    got = got.reshape(rows_of, -1, half_rows + 8, width)
    lses = got[:, :, half_rows : half_rows + 3, :half_rows].astype(jnp.float32)
    attended, _ = merged(got[:, :, :half_rows], jnp.sum(lses, axis=2))
    attended = jnp.where(live[:, None], attended, 0.0).astype(jnp.bfloat16)

    rows_in = lax.all_gather(attended[None], COL, axis=0, tiled=True)
    terms = project(rows_in, weight)
    terms = lax.all_to_all(terms, ROW, split_axis=0, concat_axis=0, tiled=True)
    total = jnp.sum(terms.astype(jnp.float32), axis=0)
    return total.astype(jnp.bfloat16)[None]


def solution(mesh):
    finer = Mesh(
        mesh.devices.reshape(8, 4, mesh.shape["ctx"], mesh.shape["head"]),
        ("lib_0", "lib_1", "ctx", "head"),
    )
    return jax.shard_map(
        body,
        mesh=finer,
        in_specs=(
            P(LIB, None, "head"),
            P(LIB, "ctx", "head"),
            P(LIB, "ctx", "head"),
            P(LIB),
            P("head", LIB),
            P(LIB, None),
            P(LIB, None),
            P(LIB),
        ),
        out_specs=P("ctx", "head", LIB),
        check_vma=False,
    )
```

```python
import functools

import jax
import jax.numpy as jnp
from jax import lax
from jax.experimental import pallas as pl
from jax.experimental.pallas import tpu as pltpu
from jax.sharding import Mesh
from jax.sharding import PartitionSpec as P

ROW, COL = "lib_0", "lib_1"
LIB = (ROW, COL)
theta_base = 500000.0
EMPTY = -1e30
CHUNK = 256
MOST = 2


def shift(value, axis, by):
    n = lax.axis_size(axis)
    return lax.ppermute(value, axis, [(i, (i + by) % n) for i in range(n)])


def coded(integers):
    return (integers // 128).astype(jnp.bfloat16), (integers % 128).astype(jnp.bfloat16)


def decoded(high, low):
    return high.astype(jnp.int32) * 128 + low.astype(jnp.int32)


def attend_kernel(scale, pieces, first, last, slot_ref, q_ref, cos_ref, sin_ref, *refs):
    key_refs, value_refs, refs = refs[:pieces], refs[pieces : 2 * pieces], refs[2 * pieces :]
    if not first:
        (before_ref, before_top_ref), refs = refs[:2], refs[2:]
    out_ref, lse_ref, q_scr, tile, k_scr, v_scr, s_scr, m_scr, acc_scr, used, entry = refs
    if not last:
        acc_scr, m_scr = out_ref.at[0], lse_ref.at[0]
    prompt = pl.program_id(0)
    listed, width = cos_ref.shape[1:]
    rows = q_ref.shape[1]
    group = q_ref.shape[2] // width
    total_rows = rows * group
    tokens = tile.shape[0]
    held = key_refs[0].shape[0] // tokens
    factor = scale * 1.4426950408889634
    chunks = [slice(r, r + CHUNK) for r in range(0, total_rows, CHUNK)]

    @pl.when(prompt == 0)
    def _():
        v_scr[:, width:] = jnp.ones((2 * tokens, width), v_scr.dtype)

    for g in range(group):
        q_scr[g * rows : (g + 1) * rows] = q_ref[0, :, g * width : (g + 1) * width]
    for span in chunks:
        if first:
            m_scr[span] = jnp.full((CHUNK, width), EMPTY, jnp.float32)
        else:
            m_scr[span] = before_top_ref[0, span]

    def note(k, count):
        slot = slot_ref[prompt * listed + k]
        used[count] = slot
        entry[count] = k
        return count + jnp.where(slot >= 0, 1, 0)

    count = lax.fori_loop(0, listed, note, 0)
    pairs = (count + 1) // 2

    def fetch(refs, slot):
        def at(index):
            return pl.ds(pl.multiple_of(index * tokens, tokens), tokens)

        if pieces == 1:
            return refs[0][at(slot)]
        for d in range(pieces):

            @pl.when(slot // held == d)
            def _():
                tile[...] = refs[d][at(slot % held)]

        return tile[...]

    def score(t, carry):
        for b in range(2):
            i = jnp.minimum(2 * t + b, count - 1)
            keys = fetch(key_refs, used[i]).astype(jnp.float32)
            cosine = cos_ref[0, pl.ds(entry[i], 1), :]
            sine = sin_ref[0, pl.ds(entry[i], 1), :]
            turned = keys * cosine + pltpu.roll(keys, width // 2, 1) * sine
            k_scr[b * tokens : (b + 1) * tokens] = turned.astype(jnp.bfloat16)
        for span in chunks:
            s = lax.dot_general(
                q_scr[span],
                k_scr[...],
                (((1,), (1,)), ((), ())),
                preferred_element_type=jnp.float32,
            )
            highest = m_scr[span]
            for u in range(0, 2 * tokens, width):
                part = s[:, u : u + width]
                s_scr[t, span, u : u + width] = part
                highest = jnp.maximum(highest, part)
            m_scr[span] = highest
        return carry

    lax.fori_loop(0, pairs, score, 0)
    for span in chunks:
        m = jnp.broadcast_to(jnp.max(m_scr[span], axis=1, keepdims=True), (CHUNK, width))
        m_scr[span] = m
        if first:
            acc_scr[span] = jnp.zeros((CHUNK, 2 * width), jnp.float32)
        else:
            weight = jnp.exp2((before_top_ref[0, span] - m) * factor)
            for u in (0, width):
                acc_scr[span, u : u + width] = before_ref[0, span, u : u + width] * weight

    def weigh(t, carry):
        for b in range(2):
            i = jnp.minimum(2 * t + b, count - 1)
            values = fetch(value_refs, used[i])
            if b == 1:
                both = 2 * t + 1 < count
                values = jnp.where(both, values, jnp.zeros_like(values))
                v_scr[tokens:, width:] = jnp.where(both, 1.0, jnp.zeros((tokens, width))).astype(v_scr.dtype)
            v_scr[b * tokens : (b + 1) * tokens, :width] = values
        for span in chunks:
            m = m_scr[span]
            parts = [
                jnp.exp2((s_scr[t, span, u : u + width] - m) * factor)
                for u in range(0, 2 * tokens, width)
            ]
            weights = jnp.concatenate([p.astype(jnp.bfloat16) for p in parts], axis=1)
            acc_scr[span] += jnp.dot(weights, v_scr[...], preferred_element_type=jnp.float32)
        return carry

    lax.fori_loop(0, pairs, weigh, 0)
    if not last:
        return
    halves = out_ref.shape[0]
    part = rows // halves
    row = lax.broadcasted_iota(jnp.int32, (rows, rows), 0)
    column = lax.broadcasted_iota(jnp.int32, (rows, rows), 1)

    def line(value):
        return jnp.sum(jnp.where(row == column, value, 0.0), axis=0, keepdims=True)

    tops, totals = [], []
    for g in range(group):
        span = slice(g * rows, (g + 1) * rows)
        total = jnp.maximum(acc_scr[span, width:], 1.0)
        out = (acc_scr[span, :width] / total).astype(out_ref.dtype)
        for c in range(halves):
            out_ref[c, g, 0] = out[c * part : (c + 1) * part]
        tops.append(line(m_scr[span]))
        totals.append(line(total))
    tops, totals = jnp.concatenate(tops, axis=0), jnp.concatenate(totals, axis=0)
    lse_ref[0] = tops * scale + jnp.log(totals)


def attend(slots, query, cosine, sine, keys, values, before, halves, rows, tokens):
    prompts, _, features = query.shape
    listed, width = cosine.shape[1:]
    group = features // width
    most = MOST * len(keys)
    whole = pl.BlockSpec(memory_space=pltpu.VMEM)
    table = pl.BlockSpec((1, listed, width), lambda j, s: (j, 0, 0))
    state = [
        pl.BlockSpec((1, rows * group, w * width), lambda j, s: (j, 0, 0)) for w in (2, 1)
    ]
    if halves:
        part = rows // halves
        out = (
            jax.ShapeDtypeStruct((halves, group, prompts, part, width), jnp.bfloat16),
            jax.ShapeDtypeStruct((prompts, group, rows), jnp.float32),
        )
        out_specs = (
            pl.BlockSpec((halves, group, 1, part, width), lambda j, s: (0, 0, j, 0, 0)),
            pl.BlockSpec((1, group, rows), lambda j, s: (j, 0, 0)),
        )
    else:
        out = tuple(
            jax.ShapeDtypeStruct((prompts, rows * group, w * width), jnp.float32) for w in (2, 1)
        )
        out_specs = tuple(state)
    work = prompts * most // 2 * rows * group * tokens
    return pl.pallas_call(
        functools.partial(attend_kernel, width**-0.5, len(keys), before is None, bool(halves)),
        out_shape=out,
        grid_spec=pltpu.PrefetchScalarGridSpec(
            num_scalar_prefetch=1,
            grid=(prompts,),
            in_specs=[pl.BlockSpec((1, rows, features), lambda j, s: (j, 0, 0)), table, table]
            + [whole] * (2 * len(keys))
            + (state if before else []),
            out_specs=out_specs,
            scratch_shapes=[
                pltpu.VMEM((rows * group, width), jnp.bfloat16),
                pltpu.VMEM((tokens, width), jnp.bfloat16),
                pltpu.VMEM((2 * tokens, width), jnp.bfloat16),
                pltpu.VMEM((2 * tokens, 2 * width), jnp.bfloat16),
                pltpu.VMEM((most // 2, rows * group, 2 * tokens), jnp.float32),
                pltpu.VMEM((rows * group, width), jnp.float32),
                pltpu.VMEM((rows * group, 2 * width), jnp.float32),
                pltpu.SMEM((most + 1,), jnp.int32),
                pltpu.SMEM((most + 1,), jnp.int32),
            ],
        ),
        cost_estimate=pl.CostEstimate(
            flops=4 * work * width, bytes_accessed=8 * work, transcendentals=work
        ),
        compiler_params=pltpu.CompilerParams(vmem_limit_bytes=48 * 1024 * 1024),
    )(slots, query, cosine, sine, *keys, *values, *(before or ()))


def project_kernel(rows_ref, weight_ref, out_ref):
    columns, heads = rows_ref.shape[:2]
    left = jnp.concatenate(
        [
            jnp.concatenate([rows_ref[d, h] for h in range(heads)], axis=1)
            for d in range(columns)
        ],
        axis=0,
    )
    right = jnp.concatenate([weight_ref[h, 0] for h in range(heads)], axis=0)
    out_ref[0] = jnp.dot(left, right, preferred_element_type=jnp.float32).astype(out_ref.dtype)


def project(rows_in, weight):
    columns, heads, rows, width = rows_in.shape
    owners, out_columns = weight.shape[1], weight.shape[3]
    return pl.pallas_call(
        project_kernel,
        out_shape=jax.ShapeDtypeStruct((owners, columns * rows, out_columns), jnp.bfloat16),
        grid=(owners,),
        in_specs=[
            pl.BlockSpec((columns, heads, rows, width), lambda s: (0, 0, 0, 0)),
            pl.BlockSpec((heads, 1, width, out_columns), lambda s: (0, s, 0, 0)),
        ],
        out_specs=pl.BlockSpec((1, columns * rows, out_columns), lambda s: (s, 0, 0)),
        compiler_params=pltpu.CompilerParams(vmem_limit_bytes=32 * 1024 * 1024),
    )(rows_in, weight)


def merged(outs, lses):
    top = jnp.max(lses, axis=0)
    share = jnp.exp(lses - top)
    total = jnp.sum(share, axis=0)
    share = share / total
    out = jnp.sum(outs.astype(jnp.float32) * share[..., None], axis=0)
    return out, top + jnp.log(total)


def three_parts(value):
    first = lax.reduce_precision(value, 8, 7)
    rest = value - first
    second = lax.reduce_precision(rest, 8, 7)
    return jnp.stack([first, second, rest - second]).astype(jnp.bfloat16)


def turns(delta, width):
    half = width // 2
    inverse = theta_base ** (-2.0 * jnp.arange(half, dtype=jnp.float32) / width)
    angle = delta.astype(jnp.float32)[..., None] * inverse
    cosine, sine = jnp.cos(angle), jnp.sin(angle)
    return jnp.concatenate([cosine, cosine], axis=-1), jnp.concatenate([-sine, sine], axis=-1)


def body(
    queries, passage_keys, passage_values, offsets, out_weight, passage_list, targets, row_counts
):
    rows_of, columns = lax.axis_size(ROW), lax.axis_size(COL)
    y, x, c = lax.axis_index(ROW), lax.axis_index(COL), lax.axis_index("ctx")
    z = lax.axis_index("head")
    held, tokens, width = passage_keys.shape
    listed = passage_list.shape[1]
    prompt_rows, features = queries.shape[1:]
    group = features // width
    halves = lax.axis_size("ctx")
    half_rows = prompt_rows // halves

    behind = jnp.pad(jnp.stack(coded(offsets)), ((0, 14), (0, width - held)))
    own_keys = jnp.concatenate([passage_keys.reshape(-1, width), behind], axis=0)
    own_values = passage_values.reshape(-1, width)
    keys = [own_keys, shift(own_keys, COL, -1), None, shift(own_keys, COL, 1)]
    values = [own_values, shift(own_values, COL, -1), None, shift(own_values, COL, 1)]
    second = lax.optimization_barrier((keys[3], values[3]))[0]
    keys[2] = shift(second, COL, 1)
    second = lax.optimization_barrier((values[1], keys[1]))[0]
    values[2] = shift(second, COL, -1)

    query = lax.all_gather(queries, ROW, axis=0, tiled=True)
    asked = jnp.stack(coded(jnp.concatenate([passage_list[0], targets[0], row_counts])))
    entries = asked.shape[1]
    asked = jnp.pad(asked, ((0, 14), (0, out_weight.shape[1] - entries)))
    asked = jnp.broadcast_to(asked, (rows_of, *asked.shape))
    weight = jnp.concatenate([out_weight.reshape(group, width, -1), asked], axis=1)
    weight = lax.all_to_all(weight, ROW, split_axis=0, concat_axis=0, tiled=True)
    asked = weight[:, width : width + 2, :entries]
    asked, keys[1], keys[3] = lax.optimization_barrier((asked, keys[1], keys[3]))
    asked = decoded(asked[:, 0], asked[:, 1])
    weight = lax.all_gather(weight[None, :, :width], "head", axis=0, tiled=True)

    local = asked[:, :listed] - y * columns * held
    mine = (local >= 0) & (local < columns * held)
    ahead = (local // held - x) % columns
    within = local % held

    def tables(order, pieces):
        slots = jnp.full_like(within, -1)
        for at, d in enumerate(order):
            slots = jnp.where(mine & (ahead == d), at * held + within, slots)
        tails = jnp.stack([p[held * tokens : held * tokens + 2, :held] for p in pieces])
        near = decoded(tails[:, 0], tails[:, 1]).reshape(-1)
        same = slots[..., None] == jnp.arange(len(order) * held, dtype=jnp.int32)
        moved = asked[:, listed : 2 * listed] - jnp.sum(jnp.where(same, near, 0), axis=-1)
        return (slots.reshape(-1), *turns(moved, width))

    before = None
    for order, laid_out in (((0, 1, 3), 0), ((2,), halves)):
        pieces = [keys[d] for d in order]
        if before is not None:
            before, pieces = lax.optimization_barrier((before, pieces))
        slots, cosine, sine = tables(order, pieces)
        before = attend(
            slots, query, cosine, sine, pieces, [values[d] for d in order], before, laid_out,
            prompt_rows, tokens,
        )
    out, lse = before

    lse = jnp.transpose(lse.reshape(rows_of, group, halves, half_rows), (2, 1, 0, 3))
    swap = [(i, 1 - i) for i in range(2)]
    pick = functools.partial(lax.dynamic_index_in_dim, axis=0, keepdims=False)
    other = lax.ppermute(pick(out, 1 - c), "ctx", swap)
    other_lse = lax.ppermute(pick(lse, 1 - c), "ctx", swap)
    out, lse = merged(
        jnp.stack([pick(out, c), other]), jnp.stack([pick(lse, c), other_lse])
    )

    out = out.astype(jnp.bfloat16).reshape(group * rows_of, half_rows, width)
    parts = jnp.moveaxis(three_parts(lse.reshape(group * rows_of, half_rows)), 0, 1)
    parts = jnp.pad(parts, ((0, 0), (0, 5), (0, width - half_rows)))
    sent = jnp.concatenate([out, parts], axis=1)
    count = lax.dynamic_index_in_dim(asked[:, 2 * listed], z, keepdims=False)
    live = c * half_rows + jnp.arange(half_rows, dtype=jnp.int32) < count
    sent, live = lax.optimization_barrier((sent, live))
    got = lax.all_to_all(sent, (ROW, "head"), split_axis=0, concat_axis=0, tiled=True)
    got, weight = lax.optimization_barrier((got, weight))
    got = got.reshape(rows_of, -1, half_rows + 8, width)
    lses = got[:, :, half_rows : half_rows + 3, :half_rows].astype(jnp.float32)
    attended, _ = merged(got[:, :, :half_rows], jnp.sum(lses, axis=2))
    attended = jnp.where(live[:, None], attended, 0.0).astype(jnp.bfloat16)

    rows_in = lax.all_gather(attended[None], COL, axis=0, tiled=True)
    terms = project(rows_in, weight)
    terms = lax.all_to_all(terms, ROW, split_axis=0, concat_axis=0, tiled=True)
    total = jnp.sum(terms.astype(jnp.float32), axis=0)
    return total.astype(jnp.bfloat16)[None]


def solution(mesh):
    finer = Mesh(
        mesh.devices.reshape(8, 4, mesh.shape["ctx"], mesh.shape["head"]),
        ("lib_0", "lib_1", "ctx", "head"),
    )
    return jax.shard_map(
        body,
        mesh=finer,
        in_specs=(
            P(LIB, None, "head"),
            P(LIB, "ctx", "head"),
            P(LIB, "ctx", "head"),
            P(LIB),
            P("head", LIB),
            P(LIB, None),
            P(LIB, None),
            P(LIB),
        ),
        out_specs=P("ctx", "head", LIB),
        check_vma=False,
    )
```

```python
import functools

import jax
import jax.numpy as jnp
from jax import lax
from jax.experimental import pallas as pl
from jax.experimental.pallas import tpu as pltpu
from jax.sharding import Mesh
from jax.sharding import PartitionSpec as P

ROW, COL = "lib_0", "lib_1"
LIB = (ROW, COL)
theta_base = 500000.0
EMPTY = -1e30
CHUNK = 1024
MOST = 2


def shift(value, axis, by):
    n = lax.axis_size(axis)
    return lax.ppermute(value, axis, [(i, (i + by) % n) for i in range(n)])


def coded(integers):
    return (integers // 128).astype(jnp.bfloat16), (integers % 128).astype(jnp.bfloat16)


def decoded(high, low):
    return high.astype(jnp.int32) * 128 + low.astype(jnp.int32)


def attend_kernel(scale, pieces, first, last, slot_ref, q_ref, cos_ref, sin_ref, *refs):
    key_refs, value_refs, refs = refs[:pieces], refs[pieces : 2 * pieces], refs[2 * pieces :]
    if not first:
        (before_ref, before_top_ref), refs = refs[:2], refs[2:]
    out_ref, lse_ref, q_scr, tile, k_scr, v_scr, s_scr, m_scr, acc_scr, used, entry = refs
    if not last:
        acc_scr, m_scr = out_ref.at[0], lse_ref.at[0]
    prompt = pl.program_id(0)
    listed, width = cos_ref.shape[1:]
    rows = q_ref.shape[1]
    group = q_ref.shape[2] // width
    total_rows = rows * group
    tokens = tile.shape[0]
    held = key_refs[0].shape[0] // tokens
    factor = scale * 1.4426950408889634
    chunks = [slice(r, r + CHUNK) for r in range(0, total_rows, CHUNK)]

    @pl.when(prompt == 0)
    def _():
        v_scr[:, width:] = jnp.ones((2 * tokens, width), v_scr.dtype)

    for g in range(group):
        q_scr[g * rows : (g + 1) * rows] = q_ref[0, :, g * width : (g + 1) * width]
    for span in chunks:
        if first:
            m_scr[span] = jnp.full((CHUNK, width), EMPTY, jnp.float32)
        else:
            m_scr[span] = before_top_ref[0, span]

    def note(k, count):
        slot = slot_ref[prompt * listed + k]
        used[count] = slot
        entry[count] = k
        return count + jnp.where(slot >= 0, 1, 0)

    count = lax.fori_loop(0, listed, note, 0)
    pairs = (count + 1) // 2

    def fetch(refs, slot):
        def at(index):
            return pl.ds(pl.multiple_of(index * tokens, tokens), tokens)

        if pieces == 1:
            return refs[0][at(slot)]
        for d in range(pieces):

            @pl.when(slot // held == d)
            def _():
                tile[...] = refs[d][at(slot % held)]

        return tile[...]

    def score(t, carry):
        for b in range(2):
            i = jnp.minimum(2 * t + b, count - 1)
            keys = fetch(key_refs, used[i]).astype(jnp.float32)
            cosine = cos_ref[0, pl.ds(entry[i], 1), :]
            sine = sin_ref[0, pl.ds(entry[i], 1), :]
            turned = keys * cosine + pltpu.roll(keys, width // 2, 1) * sine
            k_scr[b * tokens : (b + 1) * tokens] = turned.astype(jnp.bfloat16)
        for span in chunks:
            s = lax.dot_general(
                q_scr[span],
                k_scr[...],
                (((1,), (1,)), ((), ())),
                preferred_element_type=jnp.float32,
            )
            highest = m_scr[span]
            for u in range(0, 2 * tokens, width):
                part = s[:, u : u + width] * factor
                s_scr[t, span, u : u + width] = part
                highest = jnp.maximum(highest, part)
            m_scr[span] = highest
        return carry

    lax.fori_loop(0, pairs, score, 0)
    for span in chunks:
        m = jnp.broadcast_to(jnp.max(m_scr[span], axis=1, keepdims=True), (CHUNK, width))
        m_scr[span] = m
        if first:
            acc_scr[span] = jnp.zeros((CHUNK, 2 * width), jnp.float32)
        else:
            weight = jnp.exp2(before_top_ref[0, span] - m)
            for u in (0, width):
                acc_scr[span, u : u + width] = before_ref[0, span, u : u + width] * weight

    def weigh(t, carry):
        for b in range(2):
            i = jnp.minimum(2 * t + b, count - 1)
            values = fetch(value_refs, used[i])
            if b == 1:
                both = 2 * t + 1 < count
                values = jnp.where(both, values, jnp.zeros_like(values))
                v_scr[tokens:, width:] = jnp.where(both, 1.0, jnp.zeros((tokens, width))).astype(v_scr.dtype)
            v_scr[b * tokens : (b + 1) * tokens, :width] = values
        for span in chunks:
            m = m_scr[span]
            parts = [
                jnp.exp2(s_scr[t, span, u : u + width] - m)
                for u in range(0, 2 * tokens, width)
            ]
            weights = jnp.concatenate([p.astype(jnp.bfloat16) for p in parts], axis=1)
            acc_scr[span] += jnp.dot(weights, v_scr[...], preferred_element_type=jnp.float32)
        return carry

    lax.fori_loop(0, pairs, weigh, 0)
    if not last:
        return
    halves = out_ref.shape[0]
    part = rows // halves
    row = lax.broadcasted_iota(jnp.int32, (rows, rows), 0)
    column = lax.broadcasted_iota(jnp.int32, (rows, rows), 1)

    def line(value):
        return jnp.sum(jnp.where(row == column, value, 0.0), axis=0, keepdims=True)

    tops, totals = [], []
    for g in range(group):
        span = slice(g * rows, (g + 1) * rows)
        total = jnp.maximum(acc_scr[span, width:], 1.0)
        out = (acc_scr[span, :width] / total).astype(out_ref.dtype)
        for c in range(halves):
            out_ref[c, g, 0] = out[c * part : (c + 1) * part]
        tops.append(line(m_scr[span]))
        totals.append(line(total))
    tops, totals = jnp.concatenate(tops, axis=0), jnp.concatenate(totals, axis=0)
    lse_ref[0] = tops * 0.6931471805599453 + jnp.log(totals)


def attend(slots, query, cosine, sine, keys, values, before, halves, rows, tokens):
    prompts, _, features = query.shape
    listed, width = cosine.shape[1:]
    group = features // width
    most = MOST * len(keys)
    whole = pl.BlockSpec(memory_space=pltpu.VMEM)
    table = pl.BlockSpec((1, listed, width), lambda j, s: (j, 0, 0))
    state = [
        pl.BlockSpec((1, rows * group, w * width), lambda j, s: (j, 0, 0)) for w in (2, 1)
    ]
    if halves:
        part = rows // halves
        out = (
            jax.ShapeDtypeStruct((halves, group, prompts, part, width), jnp.bfloat16),
            jax.ShapeDtypeStruct((prompts, group, rows), jnp.float32),
        )
        out_specs = (
            pl.BlockSpec((halves, group, 1, part, width), lambda j, s: (0, 0, j, 0, 0)),
            pl.BlockSpec((1, group, rows), lambda j, s: (j, 0, 0)),
        )
    else:
        out = tuple(
            jax.ShapeDtypeStruct((prompts, rows * group, w * width), jnp.float32) for w in (2, 1)
        )
        out_specs = tuple(state)
    work = prompts * most // 2 * rows * group * tokens
    return pl.pallas_call(
        functools.partial(attend_kernel, width**-0.5, len(keys), before is None, bool(halves)),
        out_shape=out,
        grid_spec=pltpu.PrefetchScalarGridSpec(
            num_scalar_prefetch=1,
            grid=(prompts,),
            in_specs=[pl.BlockSpec((1, rows, features), lambda j, s: (j, 0, 0)), table, table]
            + [whole] * (2 * len(keys))
            + (state if before else []),
            out_specs=out_specs,
            scratch_shapes=[
                pltpu.VMEM((rows * group, width), jnp.bfloat16),
                pltpu.VMEM((tokens, width), jnp.bfloat16),
                pltpu.VMEM((2 * tokens, width), jnp.bfloat16),
                pltpu.VMEM((2 * tokens, 2 * width), jnp.bfloat16),
                pltpu.VMEM((most // 2, rows * group, 2 * tokens), jnp.float32),
                pltpu.VMEM((rows * group, width), jnp.float32),
                pltpu.VMEM((rows * group, 2 * width), jnp.float32),
                pltpu.SMEM((most + 1,), jnp.int32),
                pltpu.SMEM((most + 1,), jnp.int32),
            ],
        ),
        cost_estimate=pl.CostEstimate(
            flops=4 * work * width, bytes_accessed=8 * work, transcendentals=work
        ),
        compiler_params=pltpu.CompilerParams(vmem_limit_bytes=48 * 1024 * 1024),
    )(slots, query, cosine, sine, *keys, *values, *(before or ()))


def project_kernel(rows_ref, weight_ref, out_ref):
    columns, heads = rows_ref.shape[:2]
    left = jnp.concatenate(
        [
            jnp.concatenate([rows_ref[d, h] for h in range(heads)], axis=1)
            for d in range(columns)
        ],
        axis=0,
    )
    right = jnp.concatenate([weight_ref[h, 0] for h in range(heads)], axis=0)
    out_ref[0] = jnp.dot(left, right, preferred_element_type=jnp.float32).astype(out_ref.dtype)


def project(rows_in, weight):
    columns, heads, rows, width = rows_in.shape
    owners, out_columns = weight.shape[1], weight.shape[3]
    return pl.pallas_call(
        project_kernel,
        out_shape=jax.ShapeDtypeStruct((owners, columns * rows, out_columns), jnp.bfloat16),
        grid=(owners,),
        in_specs=[
            pl.BlockSpec((columns, heads, rows, width), lambda s: (0, 0, 0, 0)),
            pl.BlockSpec((heads, 1, width, out_columns), lambda s: (0, s, 0, 0)),
        ],
        out_specs=pl.BlockSpec((1, columns * rows, out_columns), lambda s: (s, 0, 0)),
        compiler_params=pltpu.CompilerParams(vmem_limit_bytes=32 * 1024 * 1024),
    )(rows_in, weight)


def merged(outs, lses):
    top = jnp.max(lses, axis=0)
    share = jnp.exp(lses - top)
    total = jnp.sum(share, axis=0)
    share = share / total
    out = jnp.sum(outs.astype(jnp.float32) * share[..., None], axis=0)
    return out, top + jnp.log(total)


def three_parts(value):
    first = lax.reduce_precision(value, 8, 7)
    rest = value - first
    second = lax.reduce_precision(rest, 8, 7)
    return jnp.stack([first, second, rest - second]).astype(jnp.bfloat16)


def turns(delta, width):
    half = width // 2
    inverse = theta_base ** (-2.0 * jnp.arange(half, dtype=jnp.float32) / width)
    angle = delta.astype(jnp.float32)[..., None] * inverse
    cosine, sine = jnp.cos(angle), jnp.sin(angle)
    return jnp.concatenate([cosine, cosine], axis=-1), jnp.concatenate([-sine, sine], axis=-1)


def body(
    queries, passage_keys, passage_values, offsets, out_weight, passage_list, targets, row_counts
):
    rows_of, columns = lax.axis_size(ROW), lax.axis_size(COL)
    y, x, c = lax.axis_index(ROW), lax.axis_index(COL), lax.axis_index("ctx")
    z = lax.axis_index("head")
    held, tokens, width = passage_keys.shape
    listed = passage_list.shape[1]
    prompt_rows, features = queries.shape[1:]
    group = features // width
    halves = lax.axis_size("ctx")
    half_rows = prompt_rows // halves

    behind = jnp.pad(jnp.stack(coded(offsets)), ((0, 14), (0, width - held)))
    own_keys = jnp.concatenate([passage_keys.reshape(-1, width), behind], axis=0)
    own_values = passage_values.reshape(-1, width)
    keys = [own_keys, shift(own_keys, COL, -1), None, shift(own_keys, COL, 1)]
    values = [own_values, shift(own_values, COL, -1), None, shift(own_values, COL, 1)]
    second = lax.optimization_barrier((keys[3], values[3]))[0]
    keys[2] = shift(second, COL, 1)
    second = lax.optimization_barrier((values[1], keys[1]))[0]
    values[2] = shift(second, COL, -1)

    query = lax.all_gather(queries, ROW, axis=0, tiled=True)
    asked = jnp.stack(coded(jnp.concatenate([passage_list[0], targets[0], row_counts])))
    entries = asked.shape[1]
    asked = jnp.pad(asked, ((0, 14), (0, out_weight.shape[1] - entries)))
    asked = jnp.broadcast_to(asked, (rows_of, *asked.shape))
    weight = jnp.concatenate([out_weight.reshape(group, width, -1), asked], axis=1)
    weight = lax.all_to_all(weight, ROW, split_axis=0, concat_axis=0, tiled=True)
    asked = weight[:, width : width + 2, :entries]
    asked, keys[1], keys[3] = lax.optimization_barrier((asked, keys[1], keys[3]))
    asked = decoded(asked[:, 0], asked[:, 1])
    weight = lax.all_gather(weight[None, :, :width], "head", axis=0, tiled=True)

    local = asked[:, :listed] - y * columns * held
    mine = (local >= 0) & (local < columns * held)
    ahead = (local // held - x) % columns
    within = local % held

    def tables(order, pieces):
        slots = jnp.full_like(within, -1)
        for at, d in enumerate(order):
            slots = jnp.where(mine & (ahead == d), at * held + within, slots)
        tails = jnp.stack([p[held * tokens : held * tokens + 2, :held] for p in pieces])
        near = decoded(tails[:, 0], tails[:, 1]).reshape(-1)
        same = slots[..., None] == jnp.arange(len(order) * held, dtype=jnp.int32)
        moved = asked[:, listed : 2 * listed] - jnp.sum(jnp.where(same, near, 0), axis=-1)
        return (slots.reshape(-1), *turns(moved, width))

    before = None
    for order, laid_out in (((0, 1, 3), 0), ((2,), halves)):
        pieces = [keys[d] for d in order]
        if before is not None:
            before, pieces = lax.optimization_barrier((before, pieces))
        slots, cosine, sine = tables(order, pieces)
        before = attend(
            slots, query, cosine, sine, pieces, [values[d] for d in order], before, laid_out,
            prompt_rows, tokens,
        )
    out, lse = before

    lse = jnp.transpose(lse.reshape(rows_of, group, halves, half_rows), (2, 1, 0, 3))
    swap = [(i, 1 - i) for i in range(2)]
    pick = functools.partial(lax.dynamic_index_in_dim, axis=0, keepdims=False)
    other = lax.ppermute(pick(out, 1 - c), "ctx", swap)
    other_lse = lax.ppermute(pick(lse, 1 - c), "ctx", swap)
    out, lse = merged(
        jnp.stack([pick(out, c), other]), jnp.stack([pick(lse, c), other_lse])
    )

    out = out.astype(jnp.bfloat16).reshape(group * rows_of, half_rows, width)
    parts = jnp.moveaxis(three_parts(lse.reshape(group * rows_of, half_rows)), 0, 1)
    parts = jnp.pad(parts, ((0, 0), (0, 5), (0, width - half_rows)))
    sent = jnp.concatenate([out, parts], axis=1)
    count = lax.dynamic_index_in_dim(asked[:, 2 * listed], z, keepdims=False)
    live = c * half_rows + jnp.arange(half_rows, dtype=jnp.int32) < count
    sent, live = lax.optimization_barrier((sent, live))
    got = lax.all_to_all(sent, (ROW, "head"), split_axis=0, concat_axis=0, tiled=True)
    got, weight = lax.optimization_barrier((got, weight))
    got = got.reshape(rows_of, -1, half_rows + 8, width)
    lses = got[:, :, half_rows : half_rows + 3, :half_rows].astype(jnp.float32)
    attended, _ = merged(got[:, :, :half_rows], jnp.sum(lses, axis=2))
    attended = jnp.where(live[:, None], attended, 0.0).astype(jnp.bfloat16)

    rows_in = lax.all_gather(attended[None], COL, axis=0, tiled=True)
    terms = project(rows_in, weight)
    terms = lax.all_to_all(terms, ROW, split_axis=0, concat_axis=0, tiled=True)
    total = jnp.sum(terms.astype(jnp.float32), axis=0)
    return total.astype(jnp.bfloat16)[None]


def solution(mesh):
    finer = Mesh(
        mesh.devices.reshape(8, 4, mesh.shape["ctx"], mesh.shape["head"]),
        ("lib_0", "lib_1", "ctx", "head"),
    )
    return jax.shard_map(
        body,
        mesh=finer,
        in_specs=(
            P(LIB, None, "head"),
            P(LIB, "ctx", "head"),
            P(LIB, "ctx", "head"),
            P(LIB),
            P("head", LIB),
            P(LIB, None),
            P(LIB, None),
            P(LIB),
        ),
        out_specs=P("ctx", "head", LIB),
        check_vma=False,
    )
```
